256 devices in a mesh: dp: 4 (over y_lo, core), pipe: 64 (over z, x, y_hi).
Axes of the slice: x: 4, y: 4 (y_hi: 2, y_lo: 2; y = y_hi * 2 + y_lo), z: 8, core: 2. Of those that a mesh axis runs over, the one named last changes fastest.
Arguments:
- acts_in: bfloat16 [4, 64, 2, 1536, 32], P('dp', 'pipe'), may hold values from -6 to 6
- cot_in: bfloat16 [4, 64, 2, 1536, 32], P('dp', 'pipe'), may hold values from -6 to 6
- stash: bfloat16 [4, 64, 2, 2, 1536, 32], P('dp', 'pipe'), may hold values from -6 to 6
- entering: bfloat16 [4, 2, 1536, 32], P('dp'), may hold values from -6 to 6
- pattern: int32 [64, 2, 72], replicated, may hold values from 0 to 2303, as said below
- weights: bfloat16 [64, 2, 2, 72, 4096], P('pipe'), may hold values from -0.5 to 0.5
- momentum: float32 [64, 2, 2, 72, 4096], P('pipe', None, None, 'dp'), may hold values from -0.6 to 0.6
Outputs:
- forward_out: bfloat16 [4, 64, 2, 1536, 32], P('dp', 'pipe')
- backward_out: bfloat16 [4, 64, 2, 1536, 32], P('dp', 'pipe')
- weights_next: bfloat16 [64, 2, 2, 72, 4096], P('pipe', None, None, 'dp')
- momentum_next: float32 [64, 2, 2, 72, 4096], P('pipe', None, None, 'dp')
The draws below stay inside these ranges and needn't reach their ends.
Inputs may be any that keep to these rules, and one draw needn't show every extreme that they name: pattern[s, 0] lists 72 different blocks of section s's up projection, pattern[s, 1] 72 different blocks of its down projection, in no particular order.
All inputs are finite; a program needn't handle non-finite values.
Results may differ from the reference program's by a relative error of at most 0.012.
Values may be sent and summed in bfloat16 or wider, within the bound.
A program may use at most 128 MiB of HBM per device.

```python
import jax
import jax.numpy as jnp
from jax import lax

D = 1536
FF = 6144
BLOCK = 64
ROWS = 32
SECTIONS = 64
NB = 72
N_DP = 4


def draw_pattern(key, part):
    key = jax.random.fold_in(key, 7)
    total = D // BLOCK * (FF // BLOCK)
    keys = jax.random.split(key, SECTIONS * 2)
    scores = jax.vmap(lambda one_key: jax.random.permutation(one_key, total))(keys).astype(jnp.int32)
    boost = jnp.zeros((SECTIONS * 2, total), jnp.int32)
    boost = boost.at[0, total - 1].set(total).at[1, 0].set(total)
    picked = lax.top_k(scores + boost, NB)[1]
    return picked.reshape(SECTIONS, 2, NB).astype(jnp.int32)


def steps_of(own_key, extent, cuts, smallest, high):
    factor_of, own = 1.0, jax.random.fold_in(own_key, 6)
    for dim, parts in cuts:
        heights = jnp.exp(jax.random.uniform(jax.random.fold_in(own, dim), (parts,), jnp.float32, smallest / len(cuts), high / len(cuts)))
        factor_of = factor_of * jnp.repeat(heights, extent[dim] // parts).reshape([-1 if axis == dim else 1 for axis in range(len(extent))])
    return factor_of


def scatter_about(stream_key, extent, spread, bound, cuts=(), held_as=jnp.bfloat16):
    result = spread * jax.random.normal(stream_key, extent, jnp.float32)
    if cuts:
        result = result * steps_of(stream_key, extent, cuts, -0.22, 0.18)
    return jnp.clip(result, -bound, bound).astype(held_as)


def setup_inputs(seed: int = 0) -> dict:
    key_of = jax.random.split(jax.random.key(seed), 8)
    acts_in = scatter_about(key_of[0], (N_DP, SECTIONS, 2, D, ROWS), 1.0, 6.0, ((0, 4), (1, 64)))
    cot_in = scatter_about(key_of[1], (N_DP, SECTIONS, 2, D, ROWS), 1.0, 6.0, ((0, 4), (1, 64)))
    stash = scatter_about(key_of[2], (N_DP, SECTIONS, 2, 2, D, ROWS), 1.0, 6.0, ((0, 4), (1, 64)))
    entering = scatter_about(key_of[3], (N_DP, 2, D, ROWS), 1.0, 6.0, ((0, 4),))
    pattern = draw_pattern(jax.random.fold_in(key_of[7], 71), 0)
    weights = scatter_about(key_of[5], (SECTIONS, 2, 2, NB, BLOCK * BLOCK), (2 * BLOCK) ** -0.5, 0.5, ((0, 64),))
    momentum = scatter_about(key_of[6], (SECTIONS, 2, 2, NB, BLOCK * BLOCK), 0.1, 0.6, ((0, 64), (3, 4)), jnp.float32)
    return dict(acts_in=acts_in, cot_in=cot_in, stash=stash, entering=entering, pattern=pattern, weights=weights, momentum=momentum)


beta_coef = 0.9
step_size = 0.2

def gelu_exact(values):
    return jax.nn.gelu(values, approximate=False)

def ref_hidden(inputs, section_weights, section_pattern):
    blocks_d = inputs.shape[0] // BLOCK
    blocks_f = FF // BLOCK
    up_rows = section_pattern[0] // blocks_f
    up_cols = section_pattern[0] % blocks_f
    up_blocks = section_weights[0].reshape(NB, BLOCK, BLOCK).astype(jnp.float32)
    input_blocks = jnp.take(inputs.reshape(blocks_d, BLOCK, -1), up_rows, axis=0)
    terms = jnp.einsum('nij,nir->njr', up_blocks, input_blocks.astype(jnp.float32))
    preact = jax.ops.segment_sum(terms, up_cols, num_segments=blocks_f)
    hidden_act = gelu_exact(preact).astype(jnp.bfloat16)
    return (preact, hidden_act, input_blocks)

def ref_forward(inputs, section_weights, section_pattern):
    preact, hidden_act, input_blocks = ref_hidden(inputs, section_weights, section_pattern)
    blocks_d = inputs.shape[0] // BLOCK
    down_rows = section_pattern[1] // blocks_d
    down_cols = section_pattern[1] % blocks_d
    down_blocks = section_weights[1].reshape(NB, BLOCK, BLOCK).astype(jnp.float32)
    act_blocks = jnp.take(hidden_act, down_rows, axis=0).astype(jnp.float32)
    terms = jnp.einsum('nij,nir->njr', down_blocks, act_blocks)
    output = jax.ops.segment_sum(terms, down_cols, num_segments=blocks_d)
    return (inputs.astype(jnp.float32) + output.reshape(inputs.shape)).astype(jnp.bfloat16)

def ref_backward(inputs, grad_out, section_weights, section_pattern):
    preact, hidden_act, input_blocks = ref_hidden(inputs, section_weights, section_pattern)
    blocks_d = inputs.shape[0] // BLOCK
    blocks_f = FF // BLOCK
    up_rows = section_pattern[0] // blocks_f
    up_cols = section_pattern[0] % blocks_f
    down_rows = section_pattern[1] // blocks_d
    down_cols = section_pattern[1] % blocks_d
    up_blocks = section_weights[0].reshape(NB, BLOCK, BLOCK).astype(jnp.float32)
    down_blocks = section_weights[1].reshape(NB, BLOCK, BLOCK).astype(jnp.float32)
    act_blocks = jnp.take(hidden_act, down_rows, axis=0).astype(jnp.float32)
    grad_blocks = jnp.take(grad_out.reshape(blocks_d, BLOCK, -1), down_cols, axis=0).astype(jnp.float32)
    grad_act = jax.ops.segment_sum(jnp.einsum('nij,njr->nir', down_blocks, grad_blocks), down_rows, num_segments=blocks_f)
    pullback = jax.vjp(gelu_exact, preact)[1]
    grad_pre = pullback(grad_act)[0].astype(jnp.bfloat16)
    pre_blocks = jnp.take(grad_pre, up_cols, axis=0).astype(jnp.float32)
    back = jax.ops.segment_sum(jnp.einsum('nij,njr->nir', up_blocks, pre_blocks), up_rows, num_segments=blocks_d)
    grad_in = (grad_out.astype(jnp.float32) + back.reshape(grad_out.shape)).astype(jnp.bfloat16)
    grad_up = jnp.einsum('nir,njr->nij', input_blocks.astype(jnp.float32), pre_blocks).reshape(NB, -1)
    grad_down = jnp.einsum('nir,njr->nij', act_blocks, grad_blocks).reshape(NB, -1)
    return (grad_in, jnp.stack([grad_up, grad_down]))
forward_all = jax.vmap(jax.vmap(ref_forward, in_axes=(0, 0, 0)), in_axes=(0, None, None))
backward_all = jax.vmap(jax.vmap(ref_backward, in_axes=(0, 0, 0, 0)), in_axes=(0, 0, None, None))

def reference(acts_in, cot_in, stash, entering, pattern, weights, momentum):
    last = SECTIONS - 1

    def section_info(position):
        section_pattern = jnp.stack([pattern[position], pattern[last - position]])
        return (weights[position], section_pattern)

    def first_slot(position):
        section_weights, section_pattern = section_info(position)
        outputs = forward_all(acts_in[:, position], section_weights, section_pattern)
        grads_in = backward_all(stash[:, position, :, 0], cot_in[:, position], section_weights, section_pattern)[0]
        return (outputs, grads_in)
    y_first, d_first = lax.map(first_slot, jnp.arange(SECTIONS, dtype=jnp.int32))
    y_first = jnp.swapaxes(y_first, 0, 1)
    d_first = jnp.swapaxes(d_first, 0, 1)
    x_copy0 = jnp.concatenate([entering[:, None, 0], y_first[:, :-1, 0]], axis=1)
    x_copy1 = jnp.concatenate([y_first[:, 1:, 1], entering[:, None, 1]], axis=1)
    g_copy0 = jnp.concatenate([d_first[:, 1:, 0], y_first[:, last:, 0]], axis=1)
    g_copy1 = jnp.concatenate([y_first[:, :1, 1], d_first[:, :-1, 1]], axis=1)
    s_copy0 = stash[:, :, 0, 1].at[:, last].set(acts_in[:, last, 0])
    s_copy1 = stash[:, :, 1, 1].at[:, 0].set(acts_in[:, 0, 1])
    x_second = jnp.stack([x_copy0, x_copy1], axis=2)
    g_second = jnp.stack([g_copy0, g_copy1], axis=2)
    s_second = jnp.stack([s_copy0, s_copy1], axis=2)

    def second_slot(position):
        section_weights, section_pattern = section_info(position)
        outputs = forward_all(x_second[:, position], section_weights, section_pattern)
        grads_in, grads_late = backward_all(s_second[:, position], g_second[:, position], section_weights, section_pattern)
        grads_early = backward_all(stash[:, position, :, 0], cot_in[:, position], section_weights, section_pattern)[1]
        return (outputs, grads_in, lax.optimization_barrier(jnp.sum(grads_early + grads_late, axis=0)))
    y_second, d_second, local = lax.map(second_slot, jnp.arange(SECTIONS, dtype=jnp.int32))
    total = local + local[::-1, ::-1]
    momentum_next = beta_coef * momentum + total / (2 * ROWS)
    weights_next = (weights.astype(jnp.float32) - step_size * momentum_next).astype(jnp.bfloat16)
    return (jnp.swapaxes(y_second, 0, 1), jnp.swapaxes(d_second, 0, 1), weights_next, momentum_next)
```

```python
import jax
import jax.numpy as jnp
from jax import lax
from jax.experimental import pallas as pl
from jax.experimental.pallas import tpu as pltpu
from jax.sharding import PartitionSpec as P

FF = 6144
BLOCK = 64
BETA = 0.9
STEP = 0.2
UNROLL = 8
VMEM_BYTES = 56 * 2**20


def dot(left, right, dims):
    return lax.dot_general(left, right, (dims, ((), ())), preferred_element_type=jnp.float32)


def mul(left, right):
    return dot(left, right, ((1,), (0,)))


def mul_nt(left, right):
    return dot(left, right, ((1,), (1,)))


def gelu_parts(values):
    cdf = 0.5 + 0.5 * lax.erf(values * 0.7071067811865476)
    slope = cdf + values * (0.3989422804014327 * jnp.exp(-0.5 * values * values))
    return values * cdf, slope


def lanes(parts):
    zero = jnp.zeros((BLOCK, 32), jnp.bfloat16)
    return jnp.concatenate([zero if part is None else part for part in parts], axis=1)


def place(pat, copy, proj, n, blocks_d, blocks_f):
    value = pat[(copy * 2 + proj) * 72 + n]
    if proj == 0:
        r = value // blocks_f
        return r, value - r * blocks_f
    r = value // blocks_d
    return value - r * blocks_d, r


def each_block(count, body):
    def step(i, carry):
        body([i * UNROLL + u for u in range(UNROLL)])
        return carry

    lax.fori_loop(0, count // UNROLL, step, 0)


def section_pass(pat, w, wt, x, gy, pre, gh, out, copy):
    blocks_d, blocks_f, count = x.shape[1], pre.shape[0], w.shape[2]

    def up(ns):
        terms = []
        for n in ns:
            d, f = place(pat, copy, 0, n, blocks_d, blocks_f)
            terms.append((f, mul(wt[copy, 0, n], x[copy, d])))
        for f, term in terms:
            pre[f] += term

    def down(ns):
        terms = []
        for n in ns:
            d, f = place(pat, copy, 1, n, blocks_d, blocks_f)
            terms.append((f, mul(w[copy, 1, n], gy[copy, d])))
        for f, term in terms:
            gh[f] += term

    each_block(count, up)
    each_block(count, down)


def section_close(pat, w, wt, hid, gp, out, copy, fwd_lanes):
    blocks_d, blocks_f, count = out.shape[0], hid.shape[0], w.shape[2]
    lane = lax.broadcasted_iota(jnp.int32, (BLOCK, 128), 1) // 32
    fwd = (lane == fwd_lanes + copy).astype(jnp.float32).astype(jnp.bfloat16)
    own = (lane % 2 == copy).astype(jnp.float32).astype(jnp.bfloat16)

    def down(ns):
        terms = []
        for n in ns:
            d, f = place(pat, copy, 1, n, blocks_d, blocks_f)
            terms.append((d, mul(wt[copy, 1, n], hid[f] * fwd)))
        for d, term in terms:
            out[d] += term

    def up(ns):
        terms = []
        for n in ns:
            d, f = place(pat, copy, 0, n, blocks_d, blocks_f)
            terms.append((d, mul(w[copy, 0, n], gp[f] * own)))
        for d, term in terms:
            out[d] += term

    each_block(count, down)
    each_block(count, up)


def clear(ref):
    def step(i, carry):
        ref[i] = jnp.zeros(ref.shape[1:], ref.dtype)
        return carry

    lax.fori_loop(0, ref.shape[0], step, 0)


def first_kernel(pat, acts, cot, stash, w, wt, y_out, send_up, send_down, hid, gp, x, gy, pre, gh, out):
    blocks_d, blocks_f = out.shape[0], pre.shape[0]
    clear(pre)
    clear(gh)

    def load(r, carry):
        rows = pl.ds(r * BLOCK, BLOCK)
        a0, a1, c0, c1 = acts[0, rows], acts[1, rows], cot[0, rows], cot[1, rows]
        x[0, r] = lanes([a0, None, stash[0, 0, rows], None])
        x[1, r] = lanes([None, a1, None, stash[1, 0, rows]])
        gy[0, r] = lanes([None, None, c0, None])
        gy[1, r] = lanes([None, None, None, c1])
        out[r] = lanes([a0, a1, c0, c1]).astype(jnp.float32)
        return carry

    lax.fori_loop(0, blocks_d, load, 0)
    for copy in range(2):
        section_pass(pat, w, wt, x, gy, pre, gh, out, copy)

    def act(f, carry):
        hidden, slope = gelu_parts(pre[f])
        hid[f] = hidden.astype(jnp.bfloat16)
        gp[f] = (slope * gh[f]).astype(jnp.bfloat16)
        return carry

    lax.fori_loop(0, blocks_f, act, 0)
    for copy in range(2):
        section_close(pat, w, wt, hid, gp, out, copy, 0)

    half = blocks_d // 2

    def store(r, carry):
        rows = pl.ds(r * BLOCK, BLOCK)
        lo, hi = out[r].astype(jnp.bfloat16), out[r + half].astype(jnp.bfloat16)
        send_up[rows, :] = jnp.concatenate([lo[:, 0:32], lo[:, 96:128], hi[:, 0:32], hi[:, 96:128]], axis=1)
        send_down[rows, :] = jnp.concatenate([lo[:, 32:96], hi[:, 32:96]], axis=1)
        return carry

    lax.fori_loop(0, half, store, 0)

    def keep(r, carry):
        rows = pl.ds(r * BLOCK, BLOCK)
        value = out[r].astype(jnp.bfloat16)
        y_out[0, rows, :] = value[:, 0:32]
        y_out[1, rows, :] = value[:, 32:64]
        return carry

    lax.fori_loop(0, blocks_d, keep, 0)


def second_kernel(
    sections, pat, acts, cot, stash, entering, y_first, got_up, got_down, hid1, gp1, w, wt,
    forward, backward, grads, x, gy, xs, gys, hid, gp, pre, gh, out,
):
    blocks_d, blocks_f, count = out.shape[0], pre.shape[0], w.shape[2]
    me = lax.axis_index("pipe")
    at_entry, at_exit = me == 0, me == sections - 1
    clear(pre)
    clear(gh)
    half = blocks_d // 2
    row = lax.broadcasted_iota(jnp.int32, (BLOCK, BLOCK), 0)
    col = lax.broadcasted_iota(jnp.int32, (BLOCK, BLOCK), 1)
    source = jnp.where(row < BLOCK // 2, 2 * row, 2 * row - BLOCK + 1)
    evens_first = (col == source).astype(jnp.float32).astype(jnp.bfloat16)

    def rearranged(value):
        return mul(evens_first, value).astype(jnp.bfloat16)

    def load(r, part):
        rows = pl.ds(r * BLOCK, BLOCK)
        sent = pl.ds((r - part * half) * BLOCK, BLOCK)
        up, down = got_up[sent, :], got_down[sent, :]
        base = part * 64
        y0, d1 = up[:, base : base + 32], up[:, base + 32 : base + 64]
        y1, d0 = down[:, base : base + 32], down[:, base + 32 : base + 64]
        x0 = jnp.where(at_entry, entering[0, rows], y0)
        x1 = jnp.where(at_exit, entering[1, rows], y1)
        g0 = jnp.where(at_exit, y_first[0, rows], d0)
        g1 = jnp.where(at_entry, y_first[1, rows], d1)
        s0 = jnp.where(at_exit, acts[0, rows], stash[0, 1, rows])
        s1 = jnp.where(at_entry, acts[1, rows], stash[1, 1, rows])
        x[0, r] = lanes([s0, None, x0, None])
        x[1, r] = lanes([None, s1, None, x1])
        gy[0, r] = lanes([g0, None, None, None])
        gy[1, r] = lanes([None, g1, None, None])
        gys[0, r] = lanes([g0, None, cot[0, rows], None])
        gys[1, r] = lanes([None, g1, None, cot[1, rows]])
        xs[0, r] = rearranged(lanes([s0, None, stash[0, 0, rows], None]))
        xs[1, r] = rearranged(lanes([None, s1, None, stash[1, 0, rows]]))
        out[r] = lanes([g0, g1, x0, x1]).astype(jnp.float32)

    for part in range(2):
        lax.fori_loop(part * half, (part + 1) * half, lambda r, carry: (load(r, part), carry)[1], 0)
    for copy in range(2):
        section_pass(pat, w, wt, x, gy, pre, gh, out, copy)

    early = lax.broadcasted_iota(jnp.int32, (BLOCK, 128), 1) >= 64

    def act(f, carry):
        hidden, slope = gelu_parts(pre[f])
        hid[f] = hidden.astype(jnp.bfloat16)
        gp[f] = (slope * gh[f]).astype(jnp.bfloat16)
        return carry

    lax.fori_loop(0, blocks_f, act, 0)
    for copy in range(2):
        section_close(pat, w, wt, hid, gp, out, copy, 2)

    def store(r, carry):
        rows = pl.ds(r * BLOCK, BLOCK)
        value = out[r].astype(jnp.bfloat16)
        for copy in range(2):
            backward[copy, rows, :] = value[:, 32 * copy : 32 * copy + 32]
            forward[copy, rows, :] = value[:, 64 + 32 * copy : 96 + 32 * copy]
        return carry

    lax.fori_loop(0, blocks_d, store, 0)

    def join(f, carry):
        gp[f] = jnp.where(early, gp1[f].astype(jnp.float32), gp[f].astype(jnp.float32)).astype(jnp.bfloat16)
        both = jnp.where(early, hid1[f].astype(jnp.float32), hid[f].astype(jnp.float32)).astype(jnp.bfloat16)
        hid[f] = rearranged(both)
        return carry

    lax.fori_loop(0, blocks_f, join, 0)

    def two_wide(value):
        return jnp.concatenate([value[: BLOCK // 2], value[BLOCK // 2 :]], axis=1).astype(jnp.bfloat16)

    for copy in range(2):

        def outer(ns, copy=copy):
            for n in ns:
                d, f = place(pat, copy, 0, n, blocks_d, blocks_f)
                grads[copy, 0, n] = two_wide(mul_nt(xs[copy, d], gp[f]))
            for n in ns:
                d, f = place(pat, copy, 1, n, blocks_d, blocks_f)
                grads[copy, 1, n] = two_wide(mul_nt(hid[f], gys[copy, d]))

        each_block(count, outer)


def call(kernel, args, outs, scratch):
    smem, vmem = pl.BlockSpec(memory_space=pltpu.SMEM), pl.BlockSpec(memory_space=pltpu.VMEM)
    return pl.pallas_call(
        kernel,
        out_shape=[jax.ShapeDtypeStruct(*out) for out in outs],
        in_specs=[smem] + [vmem] * (len(args) - 1),
        out_specs=[vmem] * len(outs),
        scratch_shapes=[pltpu.VMEM(*one) for one in scratch],
        compiler_params=pltpu.CompilerParams(vmem_limit_bytes=VMEM_BYTES),
    )(*args)


def shards(acts_in, cot_in, stash, entering, pattern, weights, momentum):
    bf16, f32 = jnp.bfloat16, jnp.float32
    me, sections = lax.axis_index("pipe"), lax.axis_size("pipe")
    group = lax.axis_index("dp")
    acts, cot, saved, fresh = acts_in[0, 0], cot_in[0, 0], stash[0, 0], entering[0]
    pat = jnp.stack(
        [
            lax.dynamic_index_in_dim(pattern, me, 0, keepdims=False),
            lax.dynamic_index_in_dim(pattern, sections - 1 - me, 0, keepdims=False),
        ]
    ).reshape(-1)
    width, tokens = acts.shape[1:]
    count = weights.shape[3]
    blocks_d, blocks_f = width // BLOCK, FF // BLOCK
    w = weights[0].reshape(2, 2, count, BLOCK, BLOCK)
    wt = jnp.swapaxes(w, 3, 4)
    d_block, f_block = (blocks_d, BLOCK, 128), (blocks_f, BLOCK, 128)
    y_first, send_up, send_down, hid, gp = call(
        first_kernel,
        (pat, acts, cot, saved, w, wt),
        [
            (acts.shape, bf16),
            ((width // 2, 128), bf16),
            ((width // 2, 128), bf16),
            (f_block, bf16),
            (f_block, bf16),
        ],
        [((2, *d_block), bf16), ((2, *d_block), bf16), (f_block, f32), (f_block, f32), (d_block, f32)],
    )
    got_up = lax.ppermute(send_up, "pipe", [(i, i + 1) for i in range(sections - 1)])
    got_down = lax.ppermute(send_down, "pipe", [(i + 1, i) for i in range(sections - 1)])
    forward, backward, grads = call(
        lambda *refs: second_kernel(sections, *refs),
        (pat, acts, cot, saved, fresh, y_first, got_up, got_down, hid, gp, w, wt),
        [(acts.shape, bf16), (acts.shape, bf16), ((2, 2, count, BLOCK // 2, 128), bf16)],
        [((2, *d_block), bf16)] * 4 + [(f_block, bf16)] * 2 + [(f_block, f32)] * 2 + [(d_block, f32)],
    )
    quarter = count // 4
    core, side = group % 2, group // 2
    grads = grads.reshape(2, 2, 2, 2, quarter, BLOCK // 2, 128)
    given = lax.dynamic_index_in_dim(grads, 1 - core, 3, keepdims=False)
    kept = lax.dynamic_index_in_dim(grads, core, 3, keepdims=False)
    got = lax.ppermute(given, "dp", [(i, i ^ 1) for i in range(4)])
    summed = (kept.astype(f32) + got.astype(f32)).astype(bf16)
    given = lax.dynamic_index_in_dim(summed, 1 - side, 2, keepdims=False)
    kept = lax.dynamic_index_in_dim(summed, side, 2, keepdims=False)
    got = lax.ppermute(given, "dp", [(i, i ^ 2) for i in range(4)])
    share = (kept.astype(f32) + got.astype(f32)).astype(bf16)
    mirrored = lax.ppermute(share, "pipe", [(i, sections - 1 - i) for i in range(sections)])
    total = share.astype(f32) + mirrored[::-1].astype(f32)
    total = total.reshape(2, 2, quarter, -1)
    momentum_next = BETA * momentum[0] + total / (2 * tokens)
    own = lax.dynamic_slice_in_dim(weights[0], group * quarter, quarter, axis=2)
    weights_next = (own.astype(f32) - STEP * momentum_next).astype(bf16)
    return forward[None, None], backward[None, None], weights_next[None], momentum_next[None]


def solution(mesh):
    placed = (
        P("dp", "pipe"),
        P("dp", "pipe"),
        P("dp", "pipe"),
        P("dp"),
        P(),
        P("pipe"),
        P("pipe", None, None, "dp"),
    )
    return jax.shard_map(
        shards,
        mesh=mesh,
        in_specs=placed,
        out_specs=(P("dp", "pipe"), P("dp", "pipe"), P("pipe", None, None, "dp"), P("pipe", None, None, "dp")),
        check_vma=False,
    )
```

```python
import jax
import jax.numpy as jnp
from jax import lax
from jax.experimental import pallas as pl
from jax.experimental.pallas import tpu as pltpu
from jax.sharding import PartitionSpec as P

FF = 6144
BLOCK = 64
BETA = 0.9
STEP = 0.2
UNROLL = 8
VMEM_BYTES = 56 * 2**20


def dot(left, right, dims):
    return lax.dot_general(left, right, (dims, ((), ())), preferred_element_type=jnp.float32)


def mul(left, right):
    return dot(left, right, ((1,), (0,)))


def mul_nt(left, right):
    return dot(left, right, ((1,), (1,)))


def gelu_parts(values):
    cdf = 0.5 + 0.5 * lax.erf(values * 0.7071067811865476)
    slope = cdf + values * (0.3989422804014327 * jnp.exp(-0.5 * values * values))
    return values * cdf, slope


def lanes(parts):
    zero = jnp.zeros((BLOCK, 32), jnp.bfloat16)
    return jnp.concatenate([zero if part is None else part for part in parts], axis=1)


def place(pat, copy, proj, n, blocks_d, blocks_f):
    value = pat[(copy * 2 + proj) * 72 + n]
    if proj == 0:
        r = value // blocks_f
        return r, value - r * blocks_f
    r = value // blocks_d
    return value - r * blocks_d, r


def each_block(count, body):
    def step(i, carry):
        body([i * UNROLL + u for u in range(UNROLL)])
        return carry

    lax.fori_loop(0, count // UNROLL, step, 0)


def section_pass(pat, w, wt, x, gy, pre, gh, out, copy):
    blocks_d, blocks_f, count = x.shape[1], pre.shape[0], w.shape[2]

    def up(ns):
        terms = []
        for n in ns:
            d, f = place(pat, copy, 0, n, blocks_d, blocks_f)
            terms.append((f, mul(wt[copy, 0, n], x[copy, d])))
        for f, term in terms:
            pre[f] += term

    def down(ns):
        terms = []
        for n in ns:
            d, f = place(pat, copy, 1, n, blocks_d, blocks_f)
            terms.append((f, mul(w[copy, 1, n], gy[copy, d])))
        for f, term in terms:
            gh[f] += term

    each_block(count, up)
    each_block(count, down)


def section_close(pat, w, wt, hid, gp, out, copy, fwd_lanes):
    blocks_d, blocks_f, count = out.shape[0], hid.shape[0], w.shape[2]
    lane = lax.broadcasted_iota(jnp.int32, (BLOCK, 128), 1) // 32
    fwd = (lane == fwd_lanes + copy).astype(jnp.float32).astype(jnp.bfloat16)
    own = (lane % 2 == copy).astype(jnp.float32).astype(jnp.bfloat16)

    def down(ns):
        terms = []
        for n in ns:
            d, f = place(pat, copy, 1, n, blocks_d, blocks_f)
            terms.append((d, mul(wt[copy, 1, n], hid[f] * fwd)))
        for d, term in terms:
            out[d] += term

    def up(ns):
        terms = []
        for n in ns:
            d, f = place(pat, copy, 0, n, blocks_d, blocks_f)
            terms.append((d, mul(w[copy, 0, n], gp[f] * own)))
        for d, term in terms:
            out[d] += term

    each_block(count, down)
    each_block(count, up)


def clear(ref):
    def step(i, carry):
        ref[i] = jnp.zeros(ref.shape[1:], ref.dtype)
        return carry

    lax.fori_loop(0, ref.shape[0], step, 0)


def first_kernel(pat, acts, cot, stash, w, wt, y_out, send_up, send_down, hid, gp, x, gy, pre, gh, out):
    blocks_d, blocks_f = out.shape[0], pre.shape[0]
    clear(pre)
    clear(gh)

    def load(r, carry):
        rows = pl.ds(r * BLOCK, BLOCK)
        a0, a1, c0, c1 = acts[0, rows], acts[1, rows], cot[0, rows], cot[1, rows]
        x[0, r] = lanes([a0, None, stash[0, 0, rows], None])
        x[1, r] = lanes([None, a1, None, stash[1, 0, rows]])
        gy[0, r] = lanes([None, None, c0, None])
        gy[1, r] = lanes([None, None, None, c1])
        out[r] = lanes([a0, a1, c0, c1]).astype(jnp.float32)
        return carry

    lax.fori_loop(0, blocks_d, load, 0)
    for copy in range(2):
        section_pass(pat, w, wt, x, gy, pre, gh, out, copy)

    def act(f, carry):
        hidden, slope = gelu_parts(pre[f])
        hid[f] = hidden.astype(jnp.bfloat16)
        gp[f] = (slope * gh[f]).astype(jnp.bfloat16)
        return carry

    lax.fori_loop(0, blocks_f, act, 0)
    for copy in range(2):
        section_close(pat, w, wt, hid, gp, out, copy, 0)

    half = blocks_d // 2

    def store(r, carry):
        rows = pl.ds(r * BLOCK, BLOCK)
        lo, hi = out[r].astype(jnp.bfloat16), out[r + half].astype(jnp.bfloat16)
        send_up[rows, :] = jnp.concatenate([lo[:, 0:32], lo[:, 96:128], hi[:, 0:32], hi[:, 96:128]], axis=1)
        send_down[rows, :] = jnp.concatenate([lo[:, 32:96], hi[:, 32:96]], axis=1)
        return carry

    lax.fori_loop(0, half, store, 0)

    def keep(r, carry):
        rows = pl.ds(r * BLOCK, BLOCK)
        value = out[r].astype(jnp.bfloat16)
        y_out[0, rows, :] = value[:, 0:32]
        y_out[1, rows, :] = value[:, 32:64]
        return carry

    lax.fori_loop(0, blocks_d, keep, 0)


def second_kernel(
    sections, pat, acts, cot, stash, entering, y_first, got_up, got_down, hid1, gp1, w, wt,
    forward, backward, xs, gys, hid, gp, x, gy, pre, gh, out,
):
    blocks_d, blocks_f = out.shape[0], pre.shape[0]
    me = lax.axis_index("pipe")
    at_entry, at_exit = me == 0, me == sections - 1
    clear(pre)
    clear(gh)
    half = blocks_d // 2
    row = lax.broadcasted_iota(jnp.int32, (BLOCK, BLOCK), 0)
    col = lax.broadcasted_iota(jnp.int32, (BLOCK, BLOCK), 1)
    source = jnp.where(row < BLOCK // 2, 2 * row, 2 * row - BLOCK + 1)
    evens_first = (col == source).astype(jnp.float32).astype(jnp.bfloat16)

    def rearranged(value):
        return mul(evens_first, value).astype(jnp.bfloat16)

    def load(r, part):
        rows = pl.ds(r * BLOCK, BLOCK)
        sent = pl.ds((r - part * half) * BLOCK, BLOCK)
        up, down = got_up[sent, :], got_down[sent, :]
        base = part * 64
        y0, d1 = up[:, base : base + 32], up[:, base + 32 : base + 64]
        y1, d0 = down[:, base : base + 32], down[:, base + 32 : base + 64]
        x0 = jnp.where(at_entry, entering[0, rows], y0)
        x1 = jnp.where(at_exit, entering[1, rows], y1)
        g0 = jnp.where(at_exit, y_first[0, rows], d0)
        g1 = jnp.where(at_entry, y_first[1, rows], d1)
        s0 = jnp.where(at_exit, acts[0, rows], stash[0, 1, rows])
        s1 = jnp.where(at_entry, acts[1, rows], stash[1, 1, rows])
        x[0, r] = lanes([s0, None, x0, None])
        x[1, r] = lanes([None, s1, None, x1])
        gy[0, r] = lanes([g0, None, None, None])
        gy[1, r] = lanes([None, g1, None, None])
        gys[0, r] = lanes([g0, None, cot[0, rows], None])
        gys[1, r] = lanes([None, g1, None, cot[1, rows]])
        xs[0, r] = rearranged(lanes([s0, None, stash[0, 0, rows], None]))
        xs[1, r] = rearranged(lanes([None, s1, None, stash[1, 0, rows]]))
        out[r] = lanes([g0, g1, x0, x1]).astype(jnp.float32)

    for part in range(2):
        lax.fori_loop(part * half, (part + 1) * half, lambda r, carry: (load(r, part), carry)[1], 0)
    for copy in range(2):
        section_pass(pat, w, wt, x, gy, pre, gh, out, copy)

    early = lax.broadcasted_iota(jnp.int32, (BLOCK, 128), 1) >= 64

    def act(f, carry):
        hidden, slope = gelu_parts(pre[f])
        hid[f] = hidden.astype(jnp.bfloat16)
        gp[f] = (slope * gh[f]).astype(jnp.bfloat16)
        return carry

    lax.fori_loop(0, blocks_f, act, 0)
    for copy in range(2):
        section_close(pat, w, wt, hid, gp, out, copy, 2)

    def store(r, carry):
        rows = pl.ds(r * BLOCK, BLOCK)
        value = out[r].astype(jnp.bfloat16)
        for copy in range(2):
            backward[copy, rows, :] = value[:, 32 * copy : 32 * copy + 32]
            forward[copy, rows, :] = value[:, 64 + 32 * copy : 96 + 32 * copy]
        return carry

    lax.fori_loop(0, blocks_d, store, 0)

    def join(f, carry):
        gp[f] = jnp.where(early, gp1[f].astype(jnp.float32), gp[f].astype(jnp.float32)).astype(jnp.bfloat16)
        both = jnp.where(early, hid1[f].astype(jnp.float32), hid[f].astype(jnp.float32)).astype(jnp.bfloat16)
        hid[f] = rearranged(both)
        return carry

    lax.fori_loop(0, blocks_f, join, 0)


def two_wide(value):
    return jnp.concatenate([value[: BLOCK // 2], value[BLOCK // 2 :]], axis=1).astype(jnp.bfloat16)


def sum_kernel(
    sections, quarter, pat, xs, gys, hid, gp, total, grads, got_core, to_side, got_side, share, got_far, wide, *sems
):
    core_sent, core_got, side_sent, side_got, far_sent, far_got = sems
    blocks_d, blocks_f = xs.shape[1], gp.shape[0]
    me, group = lax.axis_index("pipe"), lax.axis_index("dp")
    core, side = lax.rem(group, 2), group // 2
    near, over, far = group + 1 - 2 * core, group + 2 - 4 * side, sections - 1 - me
    barrier = pltpu.get_barrier_semaphore()
    for other in ((near, me), (over, me), (group, far)):
        pl.semaphore_signal(barrier, inc=1, device_id=other, device_id_type=pl.DeviceIdType.MESH)
    pl.semaphore_wait(barrier, 3)
    half = BLOCK // 2

    def compute(j):
        copy, proj = divmod(j, 2)
        for q in range(4):

            def step(i, carry, q=q):
                for u in range(6):
                    n = i * 6 + u
                    d, f = place(pat, copy, proj, q * quarter + n, blocks_d, blocks_f)
                    if proj == 0:
                        value = mul_nt(xs[copy, d], gp[f])
                    else:
                        value = mul_nt(hid[f], gys[copy, d])
                    grads[j, q // 2, q % 2, pl.ds(pl.multiple_of(n * half, half), half)] = two_wide(value)
                return carry

            lax.fori_loop(0, quarter // 6, step, 0)

    def copies(j):
        def remote(source, target, sent, got, to):
            return pltpu.make_async_remote_copy(
                src_ref=source, dst_ref=target, send_sem=sent.at[j], recv_sem=got.at[j],
                device_id=to, device_id_type=pl.DeviceIdType.MESH,
            )

        return (
            remote(grads.at[j, :, 1 - core], got_core.at[j], core_sent, core_got, (near, me)),
            remote(to_side.at[j], got_side.at[j], side_sent, side_got, (over, me)),
            remote(share.at[j], got_far.at[j], far_sent, far_got, (group, far)),
        )

    wires = [copies(j) for j in range(4)]

    def pieces(body):
        def step(i, carry):
            body(pl.ds(pl.multiple_of(i * 64, 64), 64))
            return carry

        lax.fori_loop(0, quarter * half // 64, step, 0)

    def after_core(j):
        wires[j][0].wait_recv()

        def body(rows):
            value = grads[j, 1 - side, core, rows].astype(jnp.float32) + got_core[j, 1 - side, rows].astype(jnp.float32)
            to_side[j, rows] = value.astype(jnp.bfloat16)

        pieces(body)
        wires[j][1].start()

    def after_side(j):
        wires[j][1].wait_recv()

        def body(rows):
            value = grads[j, side, core, rows].astype(jnp.float32) + got_core[j, side, rows].astype(jnp.float32)
            share[j, rows] = (value + got_side[j, rows].astype(jnp.float32)).astype(jnp.bfloat16)

        pieces(body)
        wires[j][2].start()

    def after_far(j):
        wires[j][2].wait_recv()
        mine = (j + 2) % 4
        copy, proj = divmod(mine, 2)

        def body(rows):
            wide[rows, :] = share[mine, rows].astype(jnp.float32) + got_far[j, rows].astype(jnp.float32)

        pieces(body)
        for t in range(half):
            total[copy, proj, :, t * 128 : (t + 1) * 128] = wide[pl.ds(t, quarter, stride=half), :]

    for step in range(6):
        if step < 4:
            compute(step)
            wires[step][0].start()
        if 1 <= step < 5:
            after_core(step - 1)
        if 2 <= step:
            after_side(step - 2)
    for j in range(4):
        after_far(j)
    for j in range(4):
        for wire in wires[j]:
            wire.wait_send()


def call(kernel, args, outs, scratch):
    smem, vmem = pl.BlockSpec(memory_space=pltpu.SMEM), pl.BlockSpec(memory_space=pltpu.VMEM)
    return pl.pallas_call(
        kernel,
        out_shape=[jax.ShapeDtypeStruct(*out) for out in outs],
        in_specs=[smem] + [vmem] * (len(args) - 1),
        out_specs=[vmem] * len(outs),
        scratch_shapes=[pltpu.VMEM(*one) for one in scratch],
        compiler_params=pltpu.CompilerParams(vmem_limit_bytes=VMEM_BYTES),
    )(*args)


def shards(acts_in, cot_in, stash, entering, pattern, weights, momentum):
    bf16, f32 = jnp.bfloat16, jnp.float32
    me, sections = lax.axis_index("pipe"), lax.axis_size("pipe")
    group = lax.axis_index("dp")
    acts, cot, saved, fresh = acts_in[0, 0], cot_in[0, 0], stash[0, 0], entering[0]
    pat = jnp.stack(
        [
            lax.dynamic_index_in_dim(pattern, me, 0, keepdims=False),
            lax.dynamic_index_in_dim(pattern, sections - 1 - me, 0, keepdims=False),
        ]
    ).reshape(-1)
    width, tokens = acts.shape[1:]
    count = weights.shape[3]
    blocks_d, blocks_f = width // BLOCK, FF // BLOCK
    w = weights[0].reshape(2, 2, count, BLOCK, BLOCK)
    wt = jnp.swapaxes(w, 3, 4)
    d_block, f_block = (blocks_d, BLOCK, 128), (blocks_f, BLOCK, 128)
    y_first, send_up, send_down, hid, gp = call(
        first_kernel,
        (pat, acts, cot, saved, w, wt),
        [
            (acts.shape, bf16),
            ((width // 2, 128), bf16),
            ((width // 2, 128), bf16),
            (f_block, bf16),
            (f_block, bf16),
        ],
        [((2, *d_block), bf16), ((2, *d_block), bf16), (f_block, f32), (f_block, f32), (d_block, f32)],
    )
    got_up = lax.ppermute(send_up, "pipe", [(i, i + 1) for i in range(sections - 1)])
    got_down = lax.ppermute(send_down, "pipe", [(i + 1, i) for i in range(sections - 1)])
    forward, backward, xs, gys, hid, gp = call(
        lambda *refs: second_kernel(sections, *refs),
        (pat, acts, cot, saved, fresh, y_first, got_up, got_down, hid, gp, w, wt),
        [(acts.shape, bf16)] * 2 + [((2, *d_block), bf16)] * 2 + [(f_block, bf16)] * 2,
        [((2, *d_block), bf16)] * 2 + [(f_block, f32)] * 2 + [(d_block, f32)],
    )
    quarter = count // 4
    chunk = (4, quarter * BLOCK // 2, 128)
    smem, vmem = pl.BlockSpec(memory_space=pltpu.SMEM), pl.BlockSpec(memory_space=pltpu.VMEM)
    total = pl.pallas_call(
        lambda *refs: sum_kernel(sections, quarter, *refs),
        out_shape=jax.ShapeDtypeStruct((2, 2, quarter, weights.shape[4]), f32),
        in_specs=[smem] + [vmem] * 4,
        out_specs=vmem,
        scratch_shapes=[
            pltpu.VMEM((4, 2, 2, *chunk[1:]), bf16),
            pltpu.VMEM((4, 2, *chunk[1:]), bf16),
            pltpu.VMEM(chunk, bf16),
            pltpu.VMEM(chunk, bf16),
            pltpu.VMEM(chunk, bf16),
            pltpu.VMEM(chunk, bf16),
            pltpu.VMEM(chunk[1:], f32),
        ]
        + [pltpu.SemaphoreType.DMA((4,))] * 6,
        compiler_params=pltpu.CompilerParams(collective_id=0, has_side_effects=True, vmem_limit_bytes=VMEM_BYTES),
    )(pat, xs, gys, hid, gp)
    momentum_next = BETA * momentum[0] + total / (2 * tokens)
    own = lax.dynamic_slice_in_dim(weights[0], group * quarter, quarter, axis=2)
    weights_next = (own.astype(f32) - STEP * momentum_next).astype(bf16)
    return forward[None, None], backward[None, None], weights_next[None], momentum_next[None]


def solution(mesh):
    placed = (
        P("dp", "pipe"),
        P("dp", "pipe"),
        P("dp", "pipe"),
        P("dp"),
        P(),
        P("pipe"),
        P("pipe", None, None, "dp"),
    )
    return jax.shard_map(
        shards,
        mesh=mesh,
        in_specs=placed,
        out_specs=(P("dp", "pipe"), P("dp", "pipe"), P("pipe", None, None, "dp"), P("pipe", None, None, "dp")),
        check_vma=False,
    )
```

```python
import jax
import jax.numpy as jnp
from jax import lax
from jax.experimental import pallas as pl
from jax.experimental.pallas import tpu as pltpu
from jax.sharding import PartitionSpec as P

FF = 6144
BLOCK = 64
BETA = 0.9
STEP = 0.2
UNROLL = 8
VMEM_BYTES = 56 * 2**20


def dot(left, right, dims):
    return lax.dot_general(left, right, (dims, ((), ())), preferred_element_type=jnp.float32)


def mul(left, right):
    return dot(left, right, ((1,), (0,)))


def mul_nt(left, right):
    return dot(left, right, ((1,), (1,)))


def gelu_parts(values):
    cdf = 0.5 + 0.5 * lax.erf(values * 0.7071067811865476)
    slope = cdf + values * (0.3989422804014327 * jnp.exp(-0.5 * values * values))
    return values * cdf, slope


def stack_tokens(parts):
    return jnp.concatenate(parts, axis=0).T


def copy_mask(copy, rows):
    lane = lax.broadcasted_iota(jnp.int32, (rows, 128), 1) // 32
    return (lane % 2 == copy).astype(jnp.float32).astype(jnp.bfloat16)


def wide_columns(i):
    return pl.ds(pl.multiple_of(i * 128, 128), 128)


def put(ref, i, value, *lead):
    ref[(*lead, 2 * i)] = value[:BLOCK]
    ref[(*lead, 2 * i + 1)] = value[BLOCK:]


def place(pat, copy, proj, n, blocks_d, blocks_f):
    value = pat[(copy * 2 + proj) * 72 + n]
    if proj == 0:
        r = value // blocks_f
        return r, value - r * blocks_f
    r = value // blocks_d
    return value - r * blocks_d, r


def each_block(count, body):
    def step(i, carry):
        body([i * UNROLL + u for u in range(UNROLL)])
        return carry

    lax.fori_loop(0, count // UNROLL, step, 0)


def section_pass(pat, w, wt, x, gy, pre, gh, out, copy):
    blocks_d, blocks_f, count = x.shape[1], pre.shape[0], w.shape[2]

    def up(ns):
        terms = []
        for n in ns:
            d, f = place(pat, copy, 0, n, blocks_d, blocks_f)
            terms.append((f, mul(wt[copy, 0, n], x[copy, d])))
        for f, term in terms:
            pre[f] += term

    def down(ns):
        terms = []
        for n in ns:
            d, f = place(pat, copy, 1, n, blocks_d, blocks_f)
            terms.append((f, mul(w[copy, 1, n], gy[copy, d])))
        for f, term in terms:
            gh[f] += term

    each_block(count, up)
    each_block(count, down)


def section_close(pat, w, wt, hid, gp, out, copy, fwd_lanes):
    blocks_d, blocks_f, count = out.shape[0], hid.shape[0], w.shape[2]
    lane = lax.broadcasted_iota(jnp.int32, (BLOCK, 128), 1) // 32
    fwd = (lane == fwd_lanes + copy).astype(jnp.float32).astype(jnp.bfloat16)
    own = (lane % 2 == copy).astype(jnp.float32).astype(jnp.bfloat16)

    def down(ns):
        terms = []
        for n in ns:
            d, f = place(pat, copy, 1, n, blocks_d, blocks_f)
            terms.append((d, mul(wt[copy, 1, n], hid[f] * fwd)))
        for d, term in terms:
            out[d] += term

    def up(ns):
        terms = []
        for n in ns:
            d, f = place(pat, copy, 0, n, blocks_d, blocks_f)
            terms.append((d, mul(w[copy, 0, n], gp[f] * own)))
        for d, term in terms:
            out[d] += term

    each_block(count, down)
    each_block(count, up)


def clear(ref):
    def step(i, carry):
        ref[i] = jnp.zeros(ref.shape[1:], ref.dtype)
        return carry

    lax.fori_loop(0, ref.shape[0], step, 0)


def first_kernel(pat, acts, cot, stash, w, wt, send_up, send_down, hid, gp, x, gy, pre, gh, out):
    blocks_d, blocks_f = out.shape[0], pre.shape[0]
    clear(pre)
    clear(gh)
    masks = [copy_mask(copy, 128) for copy in range(2)]
    backward = lax.broadcasted_iota(jnp.int32, (128, 128), 1) >= 64

    def load(i, carry):
        cols = wide_columns(i)
        zero = jnp.zeros((64, 128), jnp.bfloat16)
        inputs = stack_tokens([acts[0, :, cols], acts[1, :, cols], stash[0, 0, :, cols], stash[1, 0, :, cols]])
        cots = stack_tokens([zero, cot[0, :, cols], cot[1, :, cols]])
        for copy in range(2):
            put(x, i, inputs * masks[copy], copy)
            put(gy, i, cots * masks[copy], copy)
        put(out, i, jnp.where(backward, cots.astype(jnp.float32), inputs.astype(jnp.float32)))
        return carry

    lax.fori_loop(0, blocks_d // 2, load, 0)
    for copy in range(2):
        section_pass(pat, w, wt, x, gy, pre, gh, out, copy)

    def act(f, carry):
        hidden, slope = gelu_parts(pre[f])
        hid[f] = hidden.astype(jnp.bfloat16)
        gp[f] = (slope * gh[f]).astype(jnp.bfloat16)
        return carry

    lax.fori_loop(0, blocks_f, act, 0)
    for copy in range(2):
        section_close(pat, w, wt, hid, gp, out, copy, 0)

    def store(i, carry):
        cols = wide_columns(i)
        value = jnp.concatenate([out[2 * i], out[2 * i + 1]], axis=0).astype(jnp.bfloat16).T
        send_up[0:32, cols] = value[0:32]
        send_up[32:64, cols] = value[96:128]
        send_down[:, cols] = value[32:96]
        return carry

    lax.fori_loop(0, blocks_d // 2, store, 0)


def second_kernel(
    sections, pat, acts, cot, stash, entering, sent_up, sent_down, got_up, got_down, hid1, gp1, w, wt,
    forward, backward, xs, gys, hid, gp, x, gy, pre, gh, out,
):
    blocks_d, blocks_f = out.shape[0], pre.shape[0]
    me = lax.axis_index("pipe")
    at_entry, at_exit = me == 0, me == sections - 1
    clear(pre)
    clear(gh)
    row = lax.broadcasted_iota(jnp.int32, (BLOCK, BLOCK), 0)
    col = lax.broadcasted_iota(jnp.int32, (BLOCK, BLOCK), 1)
    source = jnp.where(row < BLOCK // 2, 2 * row, 2 * row - BLOCK + 1)
    evens_first = (col == source).astype(jnp.float32).astype(jnp.bfloat16)
    masks = [copy_mask(copy, 128) for copy in range(2)]
    half_masks = [copy_mask(copy, BLOCK) for copy in range(2)]
    late = lax.broadcasted_iota(jnp.int32, (128, 128), 1) < 64
    late_half = lax.broadcasted_iota(jnp.int32, (BLOCK, 128), 1) < 64
    late_only = late.astype(jnp.float32).astype(jnp.bfloat16)

    def rearranged(value):
        return mul(evens_first, value).astype(jnp.bfloat16)

    def merged(first, second, mask):
        return jnp.where(mask, first.astype(jnp.float32), second.astype(jnp.float32))

    def load(i, carry):
        cols = wide_columns(i)
        x0 = jnp.where(at_entry, entering[0, :, cols], got_up[0:32, cols])
        x1 = jnp.where(at_exit, entering[1, :, cols], got_down[0:32, cols])
        g0 = jnp.where(at_exit, sent_up[0:32, cols], got_down[32:64, cols])
        g1 = jnp.where(at_entry, sent_down[0:32, cols], got_up[32:64, cols])
        s0 = jnp.where(at_exit, acts[0, :, cols], stash[0, 1, :, cols])
        s1 = jnp.where(at_entry, acts[1, :, cols], stash[1, 1, :, cols])
        inputs = stack_tokens([s0, s1, x0, x1])
        cots = stack_tokens([g0, g1, cot[0, :, cols], cot[1, :, cols]])
        saved = stack_tokens([s0, s1, stash[0, 0, :, cols], stash[1, 0, :, cols]])
        put(out, i, merged(cots, inputs, late))
        for copy in range(2):
            put(x, i, inputs * masks[copy], copy)
            put(gys, i, cots * masks[copy], copy)
            put(gy, i, cots * (masks[copy] * late_only), copy)
        for part in range(2):
            piece = rearranged(saved[part * BLOCK : (part + 1) * BLOCK])
            for copy in range(2):
                xs[copy, 2 * i + part] = piece * half_masks[copy]
        return carry

    lax.fori_loop(0, blocks_d // 2, load, 0)
    for copy in range(2):
        section_pass(pat, w, wt, x, gy, pre, gh, out, copy)

    def act(f, carry):
        hidden, slope = gelu_parts(pre[f])
        hid[f] = hidden.astype(jnp.bfloat16)
        gp[f] = (slope * gh[f]).astype(jnp.bfloat16)
        return carry

    lax.fori_loop(0, blocks_f, act, 0)
    for copy in range(2):
        section_close(pat, w, wt, hid, gp, out, copy, 2)

    def store(i, carry):
        cols = wide_columns(i)
        value = jnp.concatenate([out[2 * i], out[2 * i + 1]], axis=0).astype(jnp.bfloat16).T
        for copy in range(2):
            backward[copy, :, cols] = value[32 * copy : 32 * copy + 32]
            forward[copy, :, cols] = value[64 + 32 * copy : 96 + 32 * copy]
        return carry

    lax.fori_loop(0, blocks_d // 2, store, 0)

    def join(f, carry):
        gp[f] = merged(gp[f], gp1[f], late_half).astype(jnp.bfloat16)
        hid[f] = rearranged(merged(hid[f], hid1[f], late_half).astype(jnp.bfloat16))
        return carry

    lax.fori_loop(0, blocks_f, join, 0)


def two_wide(value):
    return jnp.concatenate([value[: BLOCK // 2], value[BLOCK // 2 :]], axis=1).astype(jnp.bfloat16)


def sum_kernel(
    sections, quarter, pat, xs, gys, hid, gp, total, grads, got_core, to_side, got_side, share, got_own, got_far, wide, *sems
):
    core_sent, core_got, side_sent, side_got, own_sent, own_got, far_sent, far_got = sems
    blocks_d, blocks_f = xs.shape[1], gp.shape[0]
    me, group = lax.axis_index("pipe"), lax.axis_index("dp")
    core, side = lax.rem(group, 2), group // 2
    near, over, far = group + 1 - 2 * core, group + 2 - 4 * side, sections - 1 - me
    barrier = pltpu.get_barrier_semaphore()
    for other in ((near, me), (over, me), (over, far)):
        pl.semaphore_signal(barrier, inc=1, device_id=other, device_id_type=pl.DeviceIdType.MESH)
    pl.semaphore_wait(barrier, 3)
    half = BLOCK // 2

    def compute(j):
        copy, proj = divmod(j, 2)
        for q in range(4):

            def step(i, carry, q=q):
                for u in range(6):
                    n = i * 6 + u
                    d, f = place(pat, copy, proj, q * quarter + n, blocks_d, blocks_f)
                    if proj == 0:
                        value = mul_nt(xs[copy, d], gp[f])
                    else:
                        value = mul_nt(hid[f], gys[copy, d])
                    grads[j, q // 2, q % 2, pl.ds(pl.multiple_of(n * half, half), half)] = two_wide(value)
                return carry

            lax.fori_loop(0, quarter // 6, step, 0)

    def copies(j):
        def remote(source, target, sent, got, to):
            return pltpu.make_async_remote_copy(
                src_ref=source, dst_ref=target, send_sem=sent.at[j], recv_sem=got.at[j],
                device_id=to, device_id_type=pl.DeviceIdType.MESH,
            )

        return (
            remote(grads.at[j, :, 1 - core], got_core.at[j], core_sent, core_got, (near, me)),
            remote(to_side.at[j], got_side.at[j], side_sent, side_got, (over, me)),
            remote(share.at[j], got_far.at[j], far_sent, far_got, (over, far)),
            remote(share.at[j], got_own.at[j], own_sent, own_got, (over, me)),
        )

    wires = [copies(j) for j in range(4)]

    def pieces(body):
        def step(i, carry):
            body(pl.ds(pl.multiple_of(i * 64, 64), 64))
            return carry

        lax.fori_loop(0, quarter * half // 64, step, 0)

    def after_core(j):
        wires[j][0].wait_recv()

        def body(rows):
            value = grads[j, side, core, rows].astype(jnp.float32) + got_core[j, side, rows].astype(jnp.float32)
            to_side[j, rows] = value.astype(jnp.bfloat16)

        pieces(body)
        wires[j][1].start()

    def after_side(j):
        wires[j][1].wait_recv()

        def body(rows):
            value = grads[j, 1 - side, core, rows].astype(jnp.float32) + got_core[j, 1 - side, rows].astype(jnp.float32)
            share[j, rows] = (value + got_side[j, rows].astype(jnp.float32)).astype(jnp.bfloat16)

        pieces(body)
        wires[j][2].start()
        wires[j][3].start()

    def after_far(copy, proj):
        own, other = copy * 2 + proj, (1 - copy) * 2 + proj
        wires[own][3].wait_recv()
        wires[other][2].wait_recv()

        def body(i, carry):
            rows = pl.ds(pl.multiple_of(i * 64, 64), 64)
            value = got_own[own, rows].astype(jnp.float32) + got_far[other, rows].astype(jnp.float32)
            wide[pl.ds(i * 128 + proj, 64, stride=2), :] = value
            return carry

        lax.fori_loop(0, quarter * half // 64, body, 0)

    def finish(copy):
        def body(n, carry):
            for t in range(half):
                total[copy, n, :, t * 128 : (t + 1) * 128] = wide[pl.ds((n * half + t) * 2, 2), :]
            return carry

        lax.fori_loop(0, quarter, body, 0)

    for step in range(6):
        if step < 4:
            compute(step)
            wires[step][0].start()
        if 1 <= step < 5:
            after_core(step - 1)
        if 2 <= step:
            after_side(step - 2)
    for copy in (1, 0):
        for proj in range(2):
            after_far(copy, proj)
        finish(copy)
    for j in range(4):
        for wire in wires[j]:
            wire.wait_send()


def call(kernel, args, outs, scratch):
    smem, vmem = pl.BlockSpec(memory_space=pltpu.SMEM), pl.BlockSpec(memory_space=pltpu.VMEM)
    return pl.pallas_call(
        kernel,
        out_shape=[jax.ShapeDtypeStruct(*out) for out in outs],
        in_specs=[smem] + [vmem] * (len(args) - 1),
        out_specs=[vmem] * len(outs),
        scratch_shapes=[pltpu.VMEM(*one) for one in scratch],
        compiler_params=pltpu.CompilerParams(vmem_limit_bytes=VMEM_BYTES),
    )(*args)


def shards(acts_in, cot_in, stash, entering, pattern, weights, momentum):
    bf16, f32 = jnp.bfloat16, jnp.float32
    me, sections = lax.axis_index("pipe"), lax.axis_size("pipe")
    group = lax.axis_index("dp")
    acts, cot, saved, fresh = (jnp.swapaxes(one, -1, -2) for one in (acts_in[0, 0], cot_in[0, 0], stash[0, 0], entering[0]))
    pat = jnp.stack(
        [
            lax.dynamic_index_in_dim(pattern, me, 0, keepdims=False),
            lax.dynamic_index_in_dim(pattern, sections - 1 - me, 0, keepdims=False),
        ]
    ).reshape(-1)
    tokens, width = acts.shape[1:]
    count = weights.shape[3]
    blocks_d, blocks_f = width // BLOCK, FF // BLOCK
    w = weights[0].reshape(2, 2, count, BLOCK, BLOCK)
    wt = jnp.swapaxes(w, 3, 4)
    d_block, f_block = (blocks_d, BLOCK, 128), (blocks_f, BLOCK, 128)
    send_up, send_down, hid, gp = call(
        first_kernel,
        (pat, acts, cot, saved, w, wt),
        [((2 * tokens, width), bf16), ((2 * tokens, width), bf16), (f_block, bf16), (f_block, bf16)],
        [((2, *d_block), bf16), ((2, *d_block), bf16), (f_block, f32), (f_block, f32), (d_block, f32)],
    )
    got_up = lax.ppermute(send_up, "pipe", [(i, i + 1) for i in range(sections - 1)])
    got_down = lax.ppermute(send_down, "pipe", [(i + 1, i) for i in range(sections - 1)])
    forward, backward, xs, gys, hid, gp = call(
        lambda *refs: second_kernel(sections, *refs),
        (pat, acts, cot, saved, fresh, send_up, send_down, got_up, got_down, hid, gp, w, wt),
        [(acts.shape, bf16)] * 2 + [((2, *d_block), bf16)] * 2 + [(f_block, bf16)] * 2,
        [((2, *d_block), bf16)] * 2 + [(f_block, f32)] * 2 + [(d_block, f32)],
    )
    quarter = count // 4
    chunk = (4, quarter * BLOCK // 2, 128)
    smem, vmem = pl.BlockSpec(memory_space=pltpu.SMEM), pl.BlockSpec(memory_space=pltpu.VMEM)
    total = pl.pallas_call(
        lambda *refs: sum_kernel(sections, quarter, *refs),
        out_shape=jax.ShapeDtypeStruct((2, quarter, 2, weights.shape[4]), f32),
        in_specs=[smem] + [vmem] * 4,
        out_specs=vmem,
        scratch_shapes=[
            pltpu.VMEM((4, 2, 2, *chunk[1:]), bf16),
            pltpu.VMEM((4, 2, *chunk[1:]), bf16),
            pltpu.VMEM(chunk, bf16),
            pltpu.VMEM(chunk, bf16),
            pltpu.VMEM(chunk, bf16),
            pltpu.VMEM(chunk, bf16),
            pltpu.VMEM(chunk, bf16),
            pltpu.VMEM((2 * chunk[1], 128), f32),
        ]
        + [pltpu.SemaphoreType.DMA((4,))] * 8,
        compiler_params=pltpu.CompilerParams(collective_id=0, has_side_effects=True, vmem_limit_bytes=VMEM_BYTES),
    )(pat, xs, gys, hid, gp)
    total = jnp.swapaxes(total, 1, 2)
    momentum_next = BETA * momentum[0] + total / (2 * tokens)
    own = lax.dynamic_slice_in_dim(weights[0], group * quarter, quarter, axis=2)
    weights_next = (own.astype(f32) - STEP * momentum_next).astype(bf16)
    forward, backward = jnp.swapaxes(forward, 1, 2), jnp.swapaxes(backward, 1, 2)
    return forward[None, None], backward[None, None], weights_next[None], momentum_next[None]


def solution(mesh):
    placed = (
        P("dp", "pipe"),
        P("dp", "pipe"),
        P("dp", "pipe"),
        P("dp"),
        P(),
        P("pipe"),
        P("pipe", None, None, "dp"),
    )
    return jax.shard_map(
        shards,
        mesh=mesh,
        in_specs=placed,
        out_specs=(P("dp", "pipe"), P("dp", "pipe"), P("pipe", None, None, "dp"), P("pipe", None, None, "dp")),
        check_vma=False,
    )
```

```python
import jax
import jax.numpy as jnp
from jax import lax
from jax.experimental import pallas as pl
from jax.experimental.pallas import tpu as pltpu
from jax.sharding import PartitionSpec as P

FF = 6144
BLOCK = 64
BETA = 0.9
STEP = 0.2
PER = 6
ACTS = 2
SLOTS = 96
VMEM_BYTES = 56 * 2**20


def dot(left, right, dims):
    return lax.dot_general(left, right, (dims, ((), ())), preferred_element_type=jnp.float32)


def mul(left, right):
    return dot(left, right, ((1,), (0,)))


def mul_nt(left, right):
    return dot(left, right, ((1,), (1,)))


def gelu_parts(values):
    cdf = 0.5 + 0.5 * lax.erf(values * 0.7071067811865476)
    slope = cdf + values * (0.3989422804014327 * jnp.exp(-0.5 * values * values))
    return values * cdf, slope


def stack_tokens(parts):
    return jnp.concatenate(parts, axis=0).T


def copy_mask(copy, rows):
    lane = lax.broadcasted_iota(jnp.int32, (rows, 128), 1) // 32
    return (lane % 2 == copy).astype(jnp.float32).astype(jnp.bfloat16)


def wide_columns(i):
    return pl.ds(pl.multiple_of(i * 128, 128), 128)


def put(ref, i, value, *lead):
    ref[(*lead, 2 * i)] = value[:BLOCK]
    ref[(*lead, 2 * i + 1)] = value[BLOCK:]


def place(pat, copy, proj, n, blocks_d, blocks_f):
    value = pat[(copy * 2 + proj) * 72 + n]
    if proj == 0:
        r = value // blocks_f
        return r, value - r * blocks_f
    r = value // blocks_d
    return value - r * blocks_d, r


def entry(lists, which, i):
    value = lists[which * SLOTS + i]
    return value % 128, (value // 128) % 32, value // 4096


def batched(trips, width, body):
    def step(i, carry):
        body(i * width)
        return carry

    lax.fori_loop(0, trips, step, 0)


def build_lists(pat, lists, flags, count, blocks_d, blocks_f):
    dummy = blocks_d * 128 + blocks_f * 4096

    def wipe(i, carry):
        for u in range(8):
            flags[i * 8 + u] = 0
        return carry

    lax.fori_loop(0, 2 * blocks_f // 8, wipe, 0)

    def fill(i, carry):
        for which in range(4):
            lists[which * SLOTS + i] = dummy
        lists[4 * SLOTS + i] = blocks_f
        return carry

    lax.fori_loop(0, SLOTS, fill, 0)

    def mark(n, carry):
        for copy in range(2):
            _, f = place(pat, copy, 0, n, blocks_d, blocks_f)
            flags[copy * blocks_f + f] = 1
        return carry

    lax.fori_loop(0, count, mark, 0)

    def mark_both(n, carry):
        for copy in range(2):
            _, f = place(pat, copy, 1, n, blocks_d, blocks_f)
            at = copy * blocks_f + f
            flags[at] = jnp.where(flags[at] > 0, 2, 0)
        return carry

    lax.fori_loop(0, count, mark_both, 0)

    def collect(n, found):
        after = []
        for which in range(4):
            copy, proj = divmod(which, 2)
            d, f = place(pat, copy, proj, n, blocks_d, blocks_f)
            active = flags[copy * blocks_f + f] == 2
            at = which * SLOTS + found[which]
            lists[at] = jnp.where(active, n + d * 128 + f * 4096, dummy)
            after.append(found[which] + jnp.where(active, 1, 0))
        return tuple(after)

    zero = jnp.int32(0)
    found = lax.fori_loop(0, count, collect, (zero,) * 4)

    def gather(f, number):
        active = jnp.maximum(flags[f], flags[blocks_f + f]) == 2
        lists[4 * SLOTS + number] = jnp.where(active, f, blocks_f)
        return number + jnp.where(active, 1, 0)

    number = lax.fori_loop(0, blocks_f, gather, zero)
    most = jnp.maximum(jnp.maximum(found[0], found[1]), jnp.maximum(found[2], found[3]))
    lists[5 * SLOTS] = (most + PER - 1) // PER
    lists[5 * SLOTS + 1] = (number + ACTS - 1) // ACTS


def prepare_weights(lists, raw, wide, w):
    count, half = raw.shape[2], BLOCK // 2

    def spread(t, carry):
        for which in range(4):
            copy, proj = divmod(which, 2)
            value = raw[copy, proj, :, pl.ds(pl.multiple_of(t * 128, 128), 128)].astype(jnp.float32)
            wide[which, pl.ds(t, count, stride=half), :] = value
        return carry

    lax.fori_loop(0, half, spread, 0)
    row = lax.broadcasted_iota(jnp.int32, (BLOCK, BLOCK), 0)
    col = lax.broadcasted_iota(jnp.int32, (BLOCK, BLOCK), 1)
    back = (row == jnp.where(col < half, 2 * col, 2 * col - BLOCK + 1)).astype(jnp.float32).astype(jnp.bfloat16)
    eye = (row == col).astype(jnp.float32).astype(jnp.bfloat16)

    def body(i):
        done = []
        for which in range(4):
            for u in range(3):
                n = entry(lists, which, i + u)[0]
                value = wide[which, pl.ds(pl.multiple_of(n * half, half), half), :]
                split = jnp.concatenate([value[:, :BLOCK], value[:, BLOCK:]], axis=0).astype(jnp.bfloat16)
                done.append((which, n, mul(back, split).astype(jnp.bfloat16)))
        for which, n, block in done:
            w[0, which // 2, which % 2, n] = block
            w[1, which // 2, which % 2, n] = mul_nt(eye, block).astype(jnp.bfloat16)

    batched(lists[5 * SLOTS] * (PER // 3), 3, body)


def section_pass(lists, w, x, gy, pre, gh):
    def body(i):
        terms = []
        for copy in range(2):
            for u in range(PER):
                n, d, f = entry(lists, 2 * copy, i + u)
                terms.append((pre, f, mul(w[1, copy, 0, n], x[copy, d])))
                n, d, f = entry(lists, 2 * copy + 1, i + u)
                terms.append((gh, f, mul(w[0, copy, 1, n], gy[copy, d])))
        for ref, f, term in terms:
            ref[f] += term

    batched(lists[5 * SLOTS], PER, body)


def section_close(lists, w, hid, gp, out, first_fwd, first_bwd):
    lane = lax.broadcasted_iota(jnp.int32, (BLOCK, 128), 1) // 32
    fwd = [(lane == first_fwd + copy).astype(jnp.float32).astype(jnp.bfloat16) for copy in range(2)]
    bwd = [(lane == first_bwd + copy).astype(jnp.float32).astype(jnp.bfloat16) for copy in range(2)]

    def body(i):
        terms = []
        for copy in range(2):
            for u in range(PER):
                n, d, f = entry(lists, 2 * copy + 1, i + u)
                terms.append((d, mul(w[1, copy, 1, n], hid[f] * fwd[copy])))
                n, d, f = entry(lists, 2 * copy, i + u)
                terms.append((d, mul(w[0, copy, 0, n], gp[f] * bwd[copy])))
        for d, term in terms:
            out[d] += term

    batched(lists[5 * SLOTS], PER, body)


def clear(lists, refs):
    def body(i):
        for u in range(ACTS):
            f = lists[4 * SLOTS + i + u]
            for ref in refs:
                ref[f] = jnp.zeros(ref.shape[1:], ref.dtype)

    batched(lists[5 * SLOTS + 1], ACTS, body)


def first_kernel(pat, acts, cot, stash, raw, send_up, send_down, hid, gp, lists, w_out, flags, wide, w, x, gy, pre, gh, out, sem):
    blocks_d, blocks_f = out.shape[0] - 1, pre.shape[0] - 1
    build_lists(pat, lists, flags, raw.shape[2], blocks_d, blocks_f)
    prepare_weights(lists, raw, wide, w)
    keep = pltpu.make_async_copy(w, w_out, sem)
    keep.start()
    clear(lists, (pre, gh))
    masks = [copy_mask(copy, 128) for copy in range(2)]
    backward = lax.broadcasted_iota(jnp.int32, (128, 128), 1) >= 64

    def load(i, carry):
        cols = wide_columns(i)
        zero = jnp.zeros((64, 128), jnp.bfloat16)
        inputs = stack_tokens([acts[0, :, cols], acts[1, :, cols], stash[0, 0, :, cols], stash[1, 0, :, cols]])
        cots = stack_tokens([zero, cot[0, :, cols], cot[1, :, cols]])
        for copy in range(2):
            put(x, i, inputs * masks[copy], copy)
            put(gy, i, cots * masks[copy], copy)
        put(out, i, jnp.where(backward, cots.astype(jnp.float32), inputs.astype(jnp.float32)))
        return carry

    lax.fori_loop(0, blocks_d // 2, load, 0)
    section_pass(lists, w, x, gy, pre, gh)

    def act(i):
        for u in range(ACTS):
            f = lists[4 * SLOTS + i + u]
            hidden, slope = gelu_parts(pre[f])
            hid[f] = hidden.astype(jnp.bfloat16)
            gp[f] = (slope * gh[f]).astype(jnp.bfloat16)

    batched(lists[5 * SLOTS + 1], ACTS, act)
    section_close(lists, w, hid, gp, out, 0, 2)

    def store(i, carry):
        cols = wide_columns(i)
        value = jnp.concatenate([out[2 * i], out[2 * i + 1]], axis=0).astype(jnp.bfloat16).T
        send_up[0:32, cols] = value[0:32]
        send_up[32:64, cols] = value[96:128]
        send_down[:, cols] = value[32:96]
        return carry

    lax.fori_loop(0, blocks_d // 2, store, 0)
    keep.wait()


def second_kernel(
    sections, lists, acts, cot, stash, entering, sent_up, sent_down, got_up, got_down, hid1, gp1, w_in,
    forward, backward, xs, gys, hid_both, gp_both, w, hid, x, gy, pre, gh, out, sem,
):
    fetch = pltpu.make_async_copy(w_in, w, sem)
    fetch.start()
    blocks_d, blocks_f = out.shape[0] - 1, pre.shape[0] - 1
    me = lax.axis_index("pipe")
    at_entry, at_exit = me == 0, me == sections - 1
    clear(lists, (pre, gh))

    def wipe(f, carry):
        hid_both[f] = jnp.zeros(hid_both.shape[1:], hid_both.dtype)
        gp_both[f] = jnp.zeros(gp_both.shape[1:], gp_both.dtype)
        return carry

    lax.fori_loop(0, blocks_f, wipe, 0, unroll=4)
    row = lax.broadcasted_iota(jnp.int32, (BLOCK, BLOCK), 0)
    col = lax.broadcasted_iota(jnp.int32, (BLOCK, BLOCK), 1)
    source = jnp.where(row < BLOCK // 2, 2 * row, 2 * row - BLOCK + 1)
    evens_first = (col == source).astype(jnp.float32).astype(jnp.bfloat16)
    masks = [copy_mask(copy, 128) for copy in range(2)]
    half_masks = [copy_mask(copy, BLOCK) for copy in range(2)]
    late = lax.broadcasted_iota(jnp.int32, (128, 128), 1) < 64
    late_half = lax.broadcasted_iota(jnp.int32, (BLOCK, 128), 1) < 64
    late_only = late.astype(jnp.float32).astype(jnp.bfloat16)

    def rearranged(value):
        return mul(evens_first, value).astype(jnp.bfloat16)

    def merged(first, second, mask):
        return jnp.where(mask, first.astype(jnp.float32), second.astype(jnp.float32))

    def load(i, carry):
        cols = wide_columns(i)
        x0 = jnp.where(at_entry, entering[0, :, cols], got_up[0:32, cols])
        x1 = jnp.where(at_exit, entering[1, :, cols], got_down[0:32, cols])
        g0 = jnp.where(at_exit, sent_up[0:32, cols], got_down[32:64, cols])
        g1 = jnp.where(at_entry, sent_down[0:32, cols], got_up[32:64, cols])
        s0 = jnp.where(at_exit, acts[0, :, cols], stash[0, 1, :, cols])
        s1 = jnp.where(at_entry, acts[1, :, cols], stash[1, 1, :, cols])
        inputs = stack_tokens([s0, s1, x0, x1])
        cots = stack_tokens([g0, g1, cot[0, :, cols], cot[1, :, cols]])
        saved = stack_tokens([s0, s1, stash[0, 0, :, cols], stash[1, 0, :, cols]])
        put(out, i, merged(cots, inputs, late))
        for copy in range(2):
            put(x, i, inputs * masks[copy], copy)
            put(gys, i, cots * masks[copy], copy)
            put(gy, i, cots * (masks[copy] * late_only), copy)
        for part in range(2):
            piece = rearranged(saved[part * BLOCK : (part + 1) * BLOCK])
            for copy in range(2):
                xs[copy, 2 * i + part] = piece * half_masks[copy]
        return carry

    lax.fori_loop(0, blocks_d // 2, load, 0)
    fetch.wait()
    section_pass(lists, w, x, gy, pre, gh)

    def act(i):
        for u in range(ACTS):
            f = lists[4 * SLOTS + i + u]
            hidden, slope = gelu_parts(pre[f])
            hid[f] = hidden.astype(jnp.bfloat16)
            gp_both[f] = merged(slope * gh[f], gp1[f], late_half).astype(jnp.bfloat16)
            hid_both[f] = rearranged(merged(hidden, hid1[f], late_half).astype(jnp.bfloat16))

    batched(lists[5 * SLOTS + 1], ACTS, act)
    section_close(lists, w, hid, gp_both, out, 2, 0)

    def store(i, carry):
        cols = wide_columns(i)
        value = jnp.concatenate([out[2 * i], out[2 * i + 1]], axis=0).astype(jnp.bfloat16).T
        for copy in range(2):
            backward[copy, :, cols] = value[32 * copy : 32 * copy + 32]
            forward[copy, :, cols] = value[64 + 32 * copy : 96 + 32 * copy]
        return carry

    lax.fori_loop(0, blocks_d // 2, store, 0)


def two_wide(value):
    return jnp.concatenate([value[: BLOCK // 2], value[BLOCK // 2 :]], axis=1).astype(jnp.bfloat16)


def sum_kernel(
    sections, quarter, pat, xs, gys, hid, gp, total, grads, got_core, to_side, got_side, share, got_own, got_far, wide, *sems
):
    core_sent, core_got, side_sent, side_got, own_sent, own_got, far_sent, far_got = sems
    blocks_d, blocks_f = xs.shape[1], gp.shape[0] - 1
    me, group = lax.axis_index("pipe"), lax.axis_index("dp")
    core, side = lax.rem(group, 2), group // 2
    near, over, far = group + 1 - 2 * core, group + 2 - 4 * side, sections - 1 - me
    barrier = pltpu.get_barrier_semaphore()
    for other in ((near, me), (over, me), (over, far)):
        pl.semaphore_signal(barrier, inc=1, device_id=other, device_id_type=pl.DeviceIdType.MESH)
    pl.semaphore_wait(barrier, 3)
    half = BLOCK // 2

    def compute(j):
        copy, proj = divmod(j, 2)
        for q in range(4):

            def step(i, carry, q=q):
                for u in range(9):
                    n = i * 9 + u
                    d, f = place(pat, copy, proj, q * quarter + n, blocks_d, blocks_f)
                    if proj == 0:
                        value = mul_nt(xs[copy, d], gp[f])
                    else:
                        value = mul_nt(hid[f], gys[copy, d])
                    grads[j, q // 2, q % 2, pl.ds(pl.multiple_of(n * half, half), half)] = two_wide(value)
                return carry

            lax.fori_loop(0, quarter // 9, step, 0)

    def copies(j):
        def remote(source, target, sent, got, to):
            return pltpu.make_async_remote_copy(
                src_ref=source, dst_ref=target, send_sem=sent.at[j], recv_sem=got.at[j],
                device_id=to, device_id_type=pl.DeviceIdType.MESH,
            )

        return (
            remote(grads.at[j, :, 1 - core], got_core.at[j], core_sent, core_got, (near, me)),
            remote(to_side.at[j], got_side.at[j], side_sent, side_got, (over, me)),
            remote(share.at[j], got_far.at[j], far_sent, far_got, (over, far)),
            remote(share.at[j], got_own.at[j], own_sent, own_got, (over, me)),
        )

    wires = [copies(j) for j in range(4)]

    def pieces(body):
        def step(i, carry):
            body(pl.ds(pl.multiple_of(i * 64, 64), 64))
            return carry

        lax.fori_loop(0, quarter * half // 64, step, 0)

    def after_core(j):
        wires[j][0].wait_recv()

        def body(rows):
            value = grads[j, side, core, rows].astype(jnp.float32) + got_core[j, side, rows].astype(jnp.float32)
            to_side[j, rows] = value.astype(jnp.bfloat16)

        pieces(body)
        wires[j][1].start()

    def after_side(j):
        wires[j][1].wait_recv()

        def body(rows):
            value = grads[j, 1 - side, core, rows].astype(jnp.float32) + got_core[j, 1 - side, rows].astype(jnp.float32)
            share[j, rows] = (value + got_side[j, rows].astype(jnp.float32)).astype(jnp.bfloat16)

        pieces(body)
        wires[j][2].start()
        wires[j][3].start()

    def after_far(copy, proj):
        own, other = copy * 2 + proj, (1 - copy) * 2 + proj
        wires[own][3].wait_recv()
        wires[other][2].wait_recv()

        def body(i, carry):
            rows = pl.ds(pl.multiple_of(i * 64, 64), 64)
            value = got_own[own, rows].astype(jnp.float32) + got_far[other, rows].astype(jnp.float32)
            wide[pl.ds(i * 128 + proj, 64, stride=2), :] = value
            return carry

        lax.fori_loop(0, quarter * half // 64, body, 0)

    def finish(copy):
        def body(n, carry):
            for t in range(half):
                total[copy, n, :, t * 128 : (t + 1) * 128] = wide[pl.ds((n * half + t) * 2, 2), :]
            return carry

        lax.fori_loop(0, quarter, body, 0)

    for step in range(6):
        if step < 4:
            compute(step)
            wires[step][0].start()
        if 1 <= step < 5:
            after_core(step - 1)
        if 2 <= step:
            after_side(step - 2)
    for copy in (1, 0):
        for proj in range(2):
            after_far(copy, proj)
        finish(copy)
    for j in range(4):
        for wire in wires[j]:
            wire.wait_send()


def call(kernel, args, outs, scratch):
    space = {"s": pltpu.SMEM, "v": pltpu.VMEM, "a": pl.ANY}
    return pl.pallas_call(
        kernel,
        out_shape=[jax.ShapeDtypeStruct(*out[1:]) for out in outs],
        in_specs=[pl.BlockSpec(memory_space=space[kind]) for kind, _ in args],
        out_specs=[pl.BlockSpec(memory_space=space[out[0]]) for out in outs],
        scratch_shapes=[space[one[0]](*one[1:]) for one in scratch] + [pltpu.SemaphoreType.DMA],
        compiler_params=pltpu.CompilerParams(vmem_limit_bytes=VMEM_BYTES),
    )(*(value for _, value in args))


def shards(acts_in, cot_in, stash, entering, pattern, weights, momentum):
    bf16, f32 = jnp.bfloat16, jnp.float32
    me, sections = lax.axis_index("pipe"), lax.axis_size("pipe")
    group = lax.axis_index("dp")
    acts, cot, saved, fresh = (jnp.swapaxes(one, -1, -2) for one in (acts_in[0, 0], cot_in[0, 0], stash[0, 0], entering[0]))
    pat = jnp.stack(
        [
            lax.dynamic_index_in_dim(pattern, me, 0, keepdims=False),
            lax.dynamic_index_in_dim(pattern, sections - 1 - me, 0, keepdims=False),
        ]
    ).reshape(-1)
    tokens, width = acts.shape[1:]
    count = weights.shape[3]
    blocks_d, blocks_f = width // BLOCK, FF // BLOCK
    raw = weights[0]
    d_block, f_block = (blocks_d, BLOCK, 128), (blocks_f + 1, BLOCK, 128)
    x_block, out_block = (2, blocks_d + 1, BLOCK, 128), (blocks_d + 1, BLOCK, 128)
    w_shape = (2, 2, 2, count, BLOCK, BLOCK)
    send_up, send_down, hid, gp, lists, w = call(
        first_kernel,
        [("s", pat), ("v", acts), ("v", cot), ("v", saved), ("v", raw)],
        [
            ("v", (2 * tokens, width), bf16),
            ("v", (2 * tokens, width), bf16),
            ("v", f_block, bf16),
            ("v", f_block, bf16),
            ("s", (5 * SLOTS + 8,), jnp.int32),
            ("a", w_shape, bf16),
        ],
        [
            ("s", (2 * blocks_f,), jnp.int32),
            ("v", (4, count * BLOCK // 2, 128), f32),
            ("v", w_shape, bf16),
            ("v", x_block, bf16),
            ("v", x_block, bf16),
            ("v", f_block, f32),
            ("v", f_block, f32),
            ("v", out_block, f32),
        ],
    )
    got_up = lax.ppermute(send_up, "pipe", [(i, i + 1) for i in range(sections - 1)])
    got_down = lax.ppermute(send_down, "pipe", [(i + 1, i) for i in range(sections - 1)])
    vectors = (acts, cot, saved, fresh, send_up, send_down, got_up, got_down, hid, gp)
    forward, backward, xs, gys, hid, gp = call(
        lambda *refs: second_kernel(sections, *refs),
        [("s", lists)] + [("v", one) for one in vectors] + [("a", w)],
        [("v", acts.shape, bf16)] * 2 + [("v", (2, *d_block), bf16)] * 2 + [("v", f_block, bf16)] * 2,
        [
            ("v", w_shape, bf16),
            ("v", f_block, bf16),
            ("v", x_block, bf16),
            ("v", x_block, bf16),
            ("v", f_block, f32),
            ("v", f_block, f32),
            ("v", out_block, f32),
        ],
    )
    quarter = count // 4
    chunk = (4, quarter * BLOCK // 2, 128)
    smem, vmem = pl.BlockSpec(memory_space=pltpu.SMEM), pl.BlockSpec(memory_space=pltpu.VMEM)
    total = pl.pallas_call(
        lambda *refs: sum_kernel(sections, quarter, *refs),
        out_shape=jax.ShapeDtypeStruct((2, quarter, 2, weights.shape[4]), f32),
        in_specs=[smem] + [vmem] * 4,
        out_specs=vmem,
        scratch_shapes=[
            pltpu.VMEM((4, 2, 2, *chunk[1:]), bf16),
            pltpu.VMEM((4, 2, *chunk[1:]), bf16),
            pltpu.VMEM(chunk, bf16),
            pltpu.VMEM(chunk, bf16),
            pltpu.VMEM(chunk, bf16),
            pltpu.VMEM(chunk, bf16),
            pltpu.VMEM(chunk, bf16),
            pltpu.VMEM((2 * chunk[1], 128), f32),
        ]
        + [pltpu.SemaphoreType.DMA((4,))] * 8,
        compiler_params=pltpu.CompilerParams(collective_id=0, has_side_effects=True, vmem_limit_bytes=VMEM_BYTES),
    )(pat, xs, gys, hid, gp)
    total = jnp.swapaxes(total, 1, 2)
    momentum_next = BETA * momentum[0] + total / (2 * tokens)
    own = lax.dynamic_slice_in_dim(weights[0], group * quarter, quarter, axis=2)
    weights_next = (own.astype(f32) - STEP * momentum_next).astype(bf16)
    forward, backward = jnp.swapaxes(forward, 1, 2), jnp.swapaxes(backward, 1, 2)
    return forward[None, None], backward[None, None], weights_next[None], momentum_next[None]


def solution(mesh):
    placed = (
        P("dp", "pipe"),
        P("dp", "pipe"),
        P("dp", "pipe"),
        P("dp"),
        P(),
        P("pipe"),
        P("pipe", None, None, "dp"),
    )
    return jax.shard_map(
        shards,
        mesh=mesh,
        in_specs=placed,
        out_specs=(P("dp", "pipe"), P("dp", "pipe"), P("pipe", None, None, "dp"), P("pipe", None, None, "dp")),
        check_vma=False,
    )
```

```python
import jax
import jax.numpy as jnp
from jax import lax
from jax.experimental import pallas as pl
from jax.experimental.pallas import tpu as pltpu
from jax.sharding import PartitionSpec as P

FF = 6144
BLOCK = 64
BETA = 0.9
STEP = 0.2
PER = 6
ACTS = 4
PITCH = 72
PARTS = 2
VMEM_BYTES = 56 * 2**20


def dot(left, right, dims):
    return lax.dot_general(left, right, (dims, ((), ())), preferred_element_type=jnp.float32)


def mul(left, right):
    return dot(left, right, ((1,), (0,)))


def mul_nt(left, right):
    return dot(left, right, ((1,), (1,)))


def gelu_parts(values):
    cdf = 0.5 + 0.5 * lax.erf(values * 0.7071067811865476)
    slope = cdf + values * (0.3989422804014327 * jnp.exp(-0.5 * values * values))
    return values * cdf, slope


def stack_tokens(parts):
    return jnp.concatenate(parts, axis=0).T


def copy_mask(copy, rows):
    lane = lax.broadcasted_iota(jnp.int32, (rows, 128), 1) // 32
    return (lane % 2 == copy).astype(jnp.float32).astype(jnp.bfloat16)


def wide_columns(i):
    return pl.ds(pl.multiple_of(i * 128, 128), 128)


def put(ref, i, value, *lead):
    ref[(*lead, 2 * i)] = value[:BLOCK]
    ref[(*lead, 2 * i + 1)] = value[BLOCK:]


def place(pat, copy, proj, n, blocks_d, blocks_f):
    value = pat[copy * 2 + proj, n]
    if proj == 0:
        r = value // blocks_f
        return r, value - r * blocks_f
    r = value // blocks_d
    return value - r * blocks_d, r


def entry(lists, which, i):
    value = lists[which, i]
    return value % 128, (value // 128) % 32, value // 4096


def batched(number, width, body):
    def step(i, carry):
        body(i * width)
        return carry

    lax.fori_loop(0, number, step, 0)


def build_lists(pat, lists, blocks_d, blocks_f):
    f32 = jnp.float32
    dummy = blocks_d * 128 + blocks_f * 4096
    value = pat[...].astype(f32)
    which = lax.broadcasted_iota(jnp.int32, (8, 128), 0)
    lane = lax.broadcasted_iota(jnp.int32, (8, 128), 1).astype(f32)
    width = jnp.where(which % 2 == 0, f32(blocks_f), f32(blocks_d))
    high = jnp.floor((value + 0.5) / width)
    low = value - high * width
    d_of, f_of = jnp.where(which % 2 == 0, high, low), jnp.where(which % 2 == 0, low, high)
    valid = value >= 0
    f_of = jnp.where(valid, f_of, -1.0 - which.astype(f32))
    f_down = jnp.transpose(jnp.concatenate([f_of] * 16, axis=0))
    square = (128, 128)
    along = lax.broadcasted_iota(jnp.int32, square, 1).astype(f32)
    down = lax.broadcasted_iota(jnp.int32, square, 0).astype(f32)
    found, touched = [], []
    for w in range(4):
        column = jnp.broadcast_to(f_down[:, (w ^ 1) : (w ^ 1) + 1], square)
        same = column == jnp.broadcast_to(f_of[w : w + 1], square)
        found.append(jnp.max(jnp.where(same, 1.0, 0.0), axis=0, keepdims=True))
        own = jnp.broadcast_to(f_down[:, w : w + 1], square) == along
        touched.append(jnp.max(jnp.where(own, 1.0, 0.0), axis=0, keepdims=True))
    both = jnp.maximum(touched[0] * touched[1], touched[2] * touched[3])
    zero = jnp.zeros((3, 128), f32)
    active = jnp.concatenate(found + [both, zero], axis=0)
    before = (down < along).astype(f32).astype(jnp.bfloat16)
    place_of = mul(active.astype(jnp.bfloat16), before)
    entries = lane + d_of * 128.0 + f_of * 4096.0 - float(dummy)
    entries = jnp.where(which < 4, entries, lane - float(blocks_f))
    spots = jnp.where(active > 0, place_of, -1.0)
    turned = jnp.transpose(jnp.concatenate([spots, entries] * 8, axis=0))
    rows = []
    for w in range(5):
        here = jnp.broadcast_to(turned[:, w : w + 1], square) == along
        given = jnp.broadcast_to(turned[:, 8 + w : 9 + w], square)
        rest = float(dummy if w < 4 else blocks_f)
        rows.append(jnp.sum(jnp.where(here, given, 0.0), axis=0, keepdims=True) + rest)
    lists[0:8, :] = jnp.concatenate(rows + [zero], axis=0).astype(jnp.int32)
    lists[8:16, :] = place_of.astype(jnp.int32)


def trips(lists):
    most = jnp.maximum(jnp.maximum(lists[8, 127], lists[9, 127]), jnp.maximum(lists[10, 127], lists[11, 127]))
    return (most + PER - 1) // PER


def act_trips(lists):
    return (lists[12, 127] + ACTS - 1) // ACTS


def prepare_weights(lists, raw, wide, w):
    count = raw.shape[2]

    def spread(t, carry):
        for which in range(4):
            copy, proj = divmod(which, 2)
            value = raw[copy, proj, :, pl.ds(pl.multiple_of(t * 128, 128), 128)].astype(jnp.float32)
            wide[which, pl.ds(2 * t, count, stride=PITCH), :] = value
            wide[which, pl.ds(2 * t + 1, count, stride=PITCH), :] = pltpu.roll(value, BLOCK, 1)
        return carry

    lax.fori_loop(0, BLOCK // 2, spread, 0)
    row = lax.broadcasted_iota(jnp.int32, (BLOCK, BLOCK), 0)
    col = lax.broadcasted_iota(jnp.int32, (BLOCK, BLOCK), 1)
    eye = (row == col).astype(jnp.float32).astype(jnp.bfloat16)

    def body(i):
        done = []
        for which in range(4):
            for u in range(PER):
                n = entry(lists, which, i + u)[0]
                block = wide[which, pl.ds(pl.multiple_of(n * PITCH, 8), BLOCK), :][:, :BLOCK].astype(jnp.bfloat16)
                done.append((which, n, block, mul_nt(eye, block)))
        for which, n, block, turned in done:
            w[0, which // 2, which % 2, n] = block
            w[1, which // 2, which % 2, n] = turned.astype(jnp.bfloat16)

    batched(trips(lists), PER, body)


def section_pass(lists, w, x, gy, pre, gh):
    def body(i):
        terms = []
        for copy in range(2):
            for u in range(PER):
                n, d, f = entry(lists, 2 * copy, i + u)
                terms.append((pre, f, mul(w[1, copy, 0, n], x[copy, d])))
                n, d, f = entry(lists, 2 * copy + 1, i + u)
                terms.append((gh, f, mul(w[0, copy, 1, n], gy[copy, d])))
        for ref, f, term in terms:
            ref[f] += term

    batched(trips(lists), PER, body)


def section_close(lists, w, hid, gp, out, first_fwd, first_bwd):
    lane = lax.broadcasted_iota(jnp.int32, (BLOCK, 128), 1) // 32
    fwd = [(lane == first_fwd + copy).astype(jnp.float32).astype(jnp.bfloat16) for copy in range(2)]
    bwd = [(lane == first_bwd + copy).astype(jnp.float32).astype(jnp.bfloat16) for copy in range(2)]

    def body(i):
        terms = []
        for copy in range(2):
            for u in range(PER):
                n, d, f = entry(lists, 2 * copy + 1, i + u)
                terms.append((d, mul(w[1, copy, 1, n], hid[f] * fwd[copy])))
                n, d, f = entry(lists, 2 * copy, i + u)
                terms.append((d, mul(w[0, copy, 0, n], gp[f] * bwd[copy])))
        for d, term in terms:
            out[d] += term

    batched(trips(lists), PER, body)


def clear(lists, refs):
    def body(i):
        for u in range(ACTS):
            f = lists[4, i + u]
            for ref in refs:
                ref[f] = jnp.zeros(ref.shape[1:], ref.dtype)

    batched(act_trips(lists), ACTS, body)


def first_kernel(pat, acts, cot, stash, raw, send_up, send_down, hid, gp, lists_out, w_out, lists, wide, w, x, gy, pre, gh, out, sem):
    blocks_d, blocks_f = out.shape[0] - 1, pre.shape[0] - 1
    build_lists(pat, lists_out, blocks_d, blocks_f)
    read = pltpu.make_async_copy(lists_out, lists, sem)
    read.start()
    read.wait()
    prepare_weights(lists, raw, wide, w)
    keep = pltpu.make_async_copy(w, w_out, sem)
    keep.start()
    clear(lists, (pre, gh))
    masks = [copy_mask(copy, 128) for copy in range(2)]
    backward = lax.broadcasted_iota(jnp.int32, (128, 128), 1) >= 64

    def load(i, carry):
        cols = wide_columns(i)
        zero = jnp.zeros((64, 128), jnp.bfloat16)
        inputs = stack_tokens([acts[0, :, cols], acts[1, :, cols], stash[0, 0, :, cols], stash[1, 0, :, cols]])
        cots = stack_tokens([zero, cot[0, :, cols], cot[1, :, cols]])
        for copy in range(2):
            put(x, i, inputs * masks[copy], copy)
            put(gy, i, cots * masks[copy], copy)
        put(out, i, jnp.where(backward, cots.astype(jnp.float32), inputs.astype(jnp.float32)))
        return carry

    lax.fori_loop(0, blocks_d // 2, load, 0)
    section_pass(lists, w, x, gy, pre, gh)

    def act(i):
        for u in range(ACTS):
            f = lists[4, i + u]
            hidden, slope = gelu_parts(pre[f])
            hid[f] = hidden.astype(jnp.bfloat16)
            gp[f] = (slope * gh[f]).astype(jnp.bfloat16)

    batched(act_trips(lists), ACTS, act)
    section_close(lists, w, hid, gp, out, 0, 2)

    def store(i, carry):
        cols = wide_columns(i)
        value = jnp.concatenate([out[2 * i], out[2 * i + 1]], axis=0).astype(jnp.bfloat16).T
        send_up[0:32, cols] = value[0:32]
        send_up[32:64, cols] = value[96:128]
        send_down[:, cols] = value[32:96]
        return carry

    lax.fori_loop(0, blocks_d // 2, store, 0)
    keep.wait()


def second_kernel(
    sections, lists, acts, cot, stash, entering, sent_up, sent_down, got_up, got_down, hid1, gp1, w_in,
    forward, backward, xs, gys, hid_both, gp_both, w, hid, x, gy, pre, gh, out, sem,
):
    fetch = pltpu.make_async_copy(w_in, w, sem)
    fetch.start()
    blocks_d, blocks_f = out.shape[0] - 1, pre.shape[0] - 1
    me = lax.axis_index("pipe")
    at_entry, at_exit = me == 0, me == sections - 1
    clear(lists, (pre, gh))

    def wipe(f, carry):
        hid_both[f] = jnp.zeros(hid_both.shape[1:], hid_both.dtype)
        gp_both[f] = jnp.zeros(gp_both.shape[1:], gp_both.dtype)
        return carry

    lax.fori_loop(0, blocks_f, wipe, 0, unroll=4)
    row = lax.broadcasted_iota(jnp.int32, (BLOCK, BLOCK), 0)
    col = lax.broadcasted_iota(jnp.int32, (BLOCK, BLOCK), 1)
    source = jnp.where(row < BLOCK // 2, 2 * row, 2 * row - BLOCK + 1)
    evens_first = (col == source).astype(jnp.float32).astype(jnp.bfloat16)
    masks = [copy_mask(copy, 128) for copy in range(2)]
    half_masks = [copy_mask(copy, BLOCK) for copy in range(2)]
    late = lax.broadcasted_iota(jnp.int32, (128, 128), 1) < 64
    late_half = lax.broadcasted_iota(jnp.int32, (BLOCK, 128), 1) < 64
    late_only = late.astype(jnp.float32).astype(jnp.bfloat16)

    def rearranged(value):
        return mul(evens_first, value).astype(jnp.bfloat16)

    def merged(first, second, mask):
        return jnp.where(mask, first.astype(jnp.float32), second.astype(jnp.float32))

    def load(i, carry):
        cols = wide_columns(i)
        x0 = jnp.where(at_entry, entering[0, :, cols], got_up[0:32, cols])
        x1 = jnp.where(at_exit, entering[1, :, cols], got_down[0:32, cols])
        g0 = jnp.where(at_exit, sent_up[0:32, cols], got_down[32:64, cols])
        g1 = jnp.where(at_entry, sent_down[0:32, cols], got_up[32:64, cols])
        s0 = jnp.where(at_exit, acts[0, :, cols], stash[0, 1, :, cols])
        s1 = jnp.where(at_entry, acts[1, :, cols], stash[1, 1, :, cols])
        inputs = stack_tokens([s0, s1, x0, x1])
        cots = stack_tokens([g0, g1, cot[0, :, cols], cot[1, :, cols]])
        saved = stack_tokens([s0, s1, stash[0, 0, :, cols], stash[1, 0, :, cols]])
        put(out, i, merged(cots, inputs, late))
        for copy in range(2):
            put(x, i, inputs * masks[copy], copy)
            put(gys, i, cots * masks[copy], copy)
            put(gy, i, cots * (masks[copy] * late_only), copy)
        for part in range(2):
            piece = rearranged(saved[part * BLOCK : (part + 1) * BLOCK])
            for copy in range(2):
                xs[copy, 2 * i + part] = piece * half_masks[copy]
        return carry

    lax.fori_loop(0, blocks_d // 2, load, 0)
    fetch.wait()
    section_pass(lists, w, x, gy, pre, gh)

    def act(i):
        for u in range(ACTS):
            f = lists[4, i + u]
            hidden, slope = gelu_parts(pre[f])
            hid[f] = hidden.astype(jnp.bfloat16)
            gp_both[f] = merged(slope * gh[f], gp1[f], late_half).astype(jnp.bfloat16)
            hid_both[f] = rearranged(merged(hidden, hid1[f], late_half).astype(jnp.bfloat16))

    batched(act_trips(lists), ACTS, act)
    section_close(lists, w, hid, gp_both, out, 2, 0)

    def store(i, carry):
        cols = wide_columns(i)
        value = jnp.concatenate([out[2 * i], out[2 * i + 1]], axis=0).astype(jnp.bfloat16).T
        for copy in range(2):
            backward[copy, :, cols] = value[32 * copy : 32 * copy + 32]
            forward[copy, :, cols] = value[64 + 32 * copy : 96 + 32 * copy]
        return carry

    lax.fori_loop(0, blocks_d // 2, store, 0)


def two_wide(value):
    return jnp.concatenate([value[: BLOCK // 2], value[BLOCK // 2 :]], axis=1).astype(jnp.bfloat16)


def sum_kernel(
    sections, quarter, pat, xs, gys, hid, gp, total, grads, got_core, to_side, got_side, share, got_own, got_far, *sems
):
    core_sent, core_got, side_sent, side_got, own_sent, own_got, far_sent, far_got = sems
    blocks_d, blocks_f = xs.shape[1], gp.shape[0] - 1
    me, group = lax.axis_index("pipe"), lax.axis_index("dp")
    core, side = lax.rem(group, 2), group // 2
    near, over, far = group + 1 - 2 * core, group + 2 - 4 * side, sections - 1 - me
    barrier = pltpu.get_barrier_semaphore()
    for other in ((near, me), (over, me), (over, far)):
        pl.semaphore_signal(barrier, inc=1, device_id=other, device_id_type=pl.DeviceIdType.MESH)
    pl.semaphore_wait(barrier, 3)
    half = BLOCK // 2

    share_rows = quarter * half // PARTS

    def compute(j):
        copy, proj, part = j // (2 * PARTS), j // PARTS % 2, j % PARTS

        def step(q, carry):
            for u in range(quarter // PARTS):
                n = part * (quarter // PARTS) + u
                d, f = place(pat, copy, proj, q * quarter + n, blocks_d, blocks_f)
                if proj == 0:
                    value = mul_nt(xs[copy, d], gp[f])
                else:
                    value = mul_nt(hid[f], gys[copy, d])
                grads[j, q // 2, q % 2, u * half : (u + 1) * half] = two_wide(value)
            return carry

        lax.fori_loop(0, 4, step, 0)

    def copies(j):
        def remote(source, target, sent, got, to):
            return pltpu.make_async_remote_copy(
                src_ref=source, dst_ref=target, send_sem=sent.at[j], recv_sem=got.at[j],
                device_id=to, device_id_type=pl.DeviceIdType.MESH,
            )

        return (
            remote(grads.at[j, :, 1 - core], got_core.at[j], core_sent, core_got, (near, me)),
            remote(to_side.at[j], got_side.at[j], side_sent, side_got, (over, me)),
            remote(share.at[j], got_far.at[j], far_sent, far_got, (over, far)),
            remote(share.at[j], got_own.at[j], own_sent, own_got, (over, me)),
        )

    wires = [copies(j) for j in range(4 * PARTS)]

    def pieces(body):
        def step(i, carry):
            body(pl.ds(pl.multiple_of(i * 96, 96), 96))
            return carry

        lax.fori_loop(0, share_rows // 96, step, 0)

    def after_core(j):
        wires[j][0].wait_recv()

        def body(rows):
            value = grads[j, side, core, rows].astype(jnp.float32) + got_core[j, side, rows].astype(jnp.float32)
            to_side[j, rows] = value.astype(jnp.bfloat16)

        pieces(body)
        wires[j][1].start()

    def after_side(j):
        wires[j][1].wait_recv()

        def body(rows):
            value = grads[j, 1 - side, core, rows].astype(jnp.float32) + got_core[j, 1 - side, rows].astype(jnp.float32)
            share[j, rows] = (value + got_side[j, rows].astype(jnp.float32)).astype(jnp.bfloat16)

        pieces(body)
        wires[j][2].start()
        wires[j][3].start()

    def after_far(copy, proj, part):
        own, other = (copy * 2 + proj) * PARTS + part, ((1 - copy) * 2 + proj) * PARTS + part
        wires[own][3].wait_recv()
        wires[other][2].wait_recv()

        def body(i, carry):
            rows = pl.ds(pl.multiple_of(i * 96, 96), 96)
            value = got_own[own, rows].astype(jnp.float32) + got_far[other, rows].astype(jnp.float32)
            total[copy, pl.ds((part * share_rows + i * 96) * 2 + proj, 96, stride=2), :] = value
            return carry

        lax.fori_loop(0, share_rows // 96, body, 0)

    number = 4 * PARTS
    for step in range(number + 2):
        if step < number:
            compute(step)
            wires[step][0].start()
        if 1 <= step < number + 1:
            after_core(step - 1)
        if 2 <= step:
            after_side(step - 2)
    for copy in (1, 0):
        for proj in range(2):
            for part in range(PARTS):
                after_far(copy, proj, part)
    for j in range(number):
        for wire in wires[j]:
            wire.wait_send()


def call(kernel, args, outs, scratch):
    space = {"s": pltpu.SMEM, "v": pltpu.VMEM, "a": pl.ANY}
    return pl.pallas_call(
        kernel,
        out_shape=[jax.ShapeDtypeStruct(*out[1:]) for out in outs],
        in_specs=[pl.BlockSpec(memory_space=space[kind]) for kind, _ in args],
        out_specs=[pl.BlockSpec(memory_space=space[out[0]]) for out in outs],
        scratch_shapes=[space[one[0]](*one[1:]) for one in scratch] + [pltpu.SemaphoreType.DMA],
        compiler_params=pltpu.CompilerParams(vmem_limit_bytes=VMEM_BYTES),
    )(*(value for _, value in args))


def dense(value):
    copies, projs, count, size = value.shape
    value = jnp.swapaxes(value, 1, 2).reshape(copies, count, projs, size // 128, 128)
    return jnp.swapaxes(value, 2, 3).reshape(copies, -1, 128)


def spread_out(value):
    value = value.reshape(2, -1, BLOCK // 2, 2, 128)
    count = value.shape[1]
    return jnp.swapaxes(jnp.swapaxes(value, 2, 3).reshape(2, count, 2, -1), 1, 2)


def shards(acts_in, cot_in, stash, entering, pattern, weights, momentum):
    bf16, f32 = jnp.bfloat16, jnp.float32
    me, sections = lax.axis_index("pipe"), lax.axis_size("pipe")
    group = lax.axis_index("dp")
    acts, cot, saved, fresh = (jnp.swapaxes(one, -1, -2) for one in (acts_in[0, 0], cot_in[0, 0], stash[0, 0], entering[0]))
    pat = jnp.concatenate(
        [
            lax.dynamic_index_in_dim(pattern, me, 0, keepdims=False),
            lax.dynamic_index_in_dim(pattern, sections - 1 - me, 0, keepdims=False),
        ]
    )
    pat = jnp.pad(pat, ((0, 4), (0, 128 - pat.shape[1])), constant_values=-1)
    tokens, width = acts.shape[1:]
    count = weights.shape[3]
    blocks_d, blocks_f = width // BLOCK, FF // BLOCK
    raw = weights[0]
    d_block, f_block = (blocks_d, BLOCK, 128), (blocks_f + 1, BLOCK, 128)
    x_block, out_block = (2, blocks_d + 1, BLOCK, 128), (blocks_d + 1, BLOCK, 128)
    w_shape = (2, 2, 2, count, BLOCK, BLOCK)
    send_up, send_down, hid, gp, lists, w = call(
        first_kernel,
        [("v", pat), ("v", acts), ("v", cot), ("v", saved), ("v", raw)],
        [
            ("v", (2 * tokens, width), bf16),
            ("v", (2 * tokens, width), bf16),
            ("v", f_block, bf16),
            ("v", f_block, bf16),
            ("v", (16, 128), jnp.int32),
            ("a", w_shape, bf16),
        ],
        [
            ("s", (16, 128), jnp.int32),
            ("v", (4, count * PITCH, 128), f32),
            ("v", w_shape, bf16),
            ("v", x_block, bf16),
            ("v", x_block, bf16),
            ("v", f_block, f32),
            ("v", f_block, f32),
            ("v", out_block, f32),
        ],
    )
    got_up = lax.ppermute(send_up, "pipe", [(i, i + 1) for i in range(sections - 1)])
    got_down = lax.ppermute(send_down, "pipe", [(i + 1, i) for i in range(sections - 1)])
    vectors = (acts, cot, saved, fresh, send_up, send_down, got_up, got_down, hid, gp)
    forward, backward, xs, gys, hid, gp = call(
        lambda *refs: second_kernel(sections, *refs),
        [("s", lists)] + [("v", one) for one in vectors] + [("a", w)],
        [("v", acts.shape, bf16)] * 2 + [("v", (2, *d_block), bf16)] * 2 + [("v", f_block, bf16)] * 2,
        [
            ("v", w_shape, bf16),
            ("v", f_block, bf16),
            ("v", x_block, bf16),
            ("v", x_block, bf16),
            ("v", f_block, f32),
            ("v", f_block, f32),
            ("v", out_block, f32),
        ],
    )
    quarter = count // 4
    chunk = (4 * PARTS, quarter * BLOCK // 2 // PARTS, 128)
    smem, vmem = pl.BlockSpec(memory_space=pltpu.SMEM), pl.BlockSpec(memory_space=pltpu.VMEM)
    total = pl.pallas_call(
        lambda *refs: sum_kernel(sections, quarter, *refs),
        out_shape=jax.ShapeDtypeStruct((2, quarter * BLOCK, 128), f32),
        in_specs=[smem] + [vmem] * 4,
        out_specs=vmem,
        scratch_shapes=[
            pltpu.VMEM((4 * PARTS, 2, 2, *chunk[1:]), bf16),
            pltpu.VMEM((4 * PARTS, 2, *chunk[1:]), bf16),
            pltpu.VMEM(chunk, bf16),
            pltpu.VMEM(chunk, bf16),
            pltpu.VMEM(chunk, bf16),
            pltpu.VMEM(chunk, bf16),
            pltpu.VMEM(chunk, bf16),
        ]
        + [pltpu.SemaphoreType.DMA((4 * PARTS,))] * 8,
        compiler_params=pltpu.CompilerParams(collective_id=0, has_side_effects=True, vmem_limit_bytes=VMEM_BYTES),
    )(pat, xs, gys, hid, gp)
    own = lax.dynamic_slice_in_dim(weights[0], group * quarter, quarter, axis=2)
    momentum_next = BETA * dense(momentum[0]) + total / (2 * tokens)
    weights_next = spread_out((dense(own).astype(f32) - STEP * momentum_next).astype(bf16))
    momentum_next = spread_out(momentum_next)
    forward, backward = jnp.swapaxes(forward, 1, 2), jnp.swapaxes(backward, 1, 2)
    return forward[None, None], backward[None, None], weights_next[None], momentum_next[None]


def solution(mesh):
    placed = (
        P("dp", "pipe"),
        P("dp", "pipe"),
        P("dp", "pipe"),
        P("dp"),
        P(),
        P("pipe"),
        P("pipe", None, None, "dp"),
    )
    return jax.shard_map(
        shards,
        mesh=mesh,
        in_specs=placed,
        out_specs=(P("dp", "pipe"), P("dp", "pipe"), P("pipe", None, None, "dp"), P("pipe", None, None, "dp")),
        check_vma=False,
    )
```

```python
import jax
import jax.numpy as jnp
from jax import lax
from jax.experimental import pallas as pl
from jax.experimental.pallas import tpu as pltpu
from jax.sharding import PartitionSpec as P

FF = 6144
BLOCK = 64
BETA = 0.9
STEP = 0.2
PER = 12
ACTS = 8
PITCH = 72
PARTS = 2
VMEM_BYTES = 56 * 2**20


def dot(left, right, dims):
    return lax.dot_general(left, right, (dims, ((), ())), preferred_element_type=jnp.float32)


def mul(left, right):
    return dot(left, right, ((1,), (0,)))


def mul_nt(left, right):
    return dot(left, right, ((1,), (1,)))


def gelu_parts(values):
    cdf = 0.5 + 0.5 * lax.erf(values * 0.7071067811865476)
    slope = cdf + values * (0.3989422804014327 * jnp.exp(-0.5 * values * values))
    return values * cdf, slope


def stack_tokens(parts):
    return jnp.concatenate(parts, axis=0).T


def copy_mask(copy, rows):
    lane = lax.broadcasted_iota(jnp.int32, (rows, 128), 1) // 32
    return (lane % 2 == copy).astype(jnp.float32).astype(jnp.bfloat16)


def wide_columns(i):
    return pl.ds(pl.multiple_of(i * 128, 128), 128)


def put(ref, i, value, *lead):
    ref[(*lead, 2 * i)] = value[:BLOCK]
    ref[(*lead, 2 * i + 1)] = value[BLOCK:]


def place(pat, copy, proj, n, blocks_d, blocks_f):
    value = pat[copy * 2 + proj, n]
    if proj == 0:
        r = value // blocks_f
        return r, value - r * blocks_f
    r = value // blocks_d
    return value - r * blocks_d, r


def entry(lists, which, i):
    value = lists[which, i]
    return value % 128, (value // 128) % 32, value // 4096


def batched(number, width, body):
    def step(i, carry):
        body(i * width)
        return carry

    lax.fori_loop(0, number, step, 0)


def begin(source, target, sem):
    copy = pltpu.make_async_copy(source, target, sem)
    copy.start()
    return copy


def build_lists(pat, lists, blocks_d, blocks_f):
    f32 = jnp.float32
    dummy = blocks_d * 128 + blocks_f * 4096
    value = pat[...].astype(f32)
    which = lax.broadcasted_iota(jnp.int32, (8, 128), 0)
    lane = lax.broadcasted_iota(jnp.int32, (8, 128), 1).astype(f32)
    width = jnp.where(which % 2 == 0, f32(blocks_f), f32(blocks_d))
    high = jnp.floor((value + 0.5) / width)
    low = value - high * width
    d_of, f_of = jnp.where(which % 2 == 0, high, low), jnp.where(which % 2 == 0, low, high)
    valid = value >= 0
    f_of = jnp.where(valid, f_of, -1.0 - which.astype(f32))
    f_down = jnp.transpose(jnp.concatenate([f_of] * 16, axis=0))
    square = (128, 128)
    along = lax.broadcasted_iota(jnp.int32, square, 1).astype(f32)
    down = lax.broadcasted_iota(jnp.int32, square, 0).astype(f32)
    found, touched = [], []
    for w in range(4):
        column = jnp.broadcast_to(f_down[:, (w ^ 1) : (w ^ 1) + 1], square)
        same = column == jnp.broadcast_to(f_of[w : w + 1], square)
        found.append(jnp.max(jnp.where(same, 1.0, 0.0), axis=0, keepdims=True))
        own = jnp.broadcast_to(f_down[:, w : w + 1], square) == along
        touched.append(jnp.max(jnp.where(own, 1.0, 0.0), axis=0, keepdims=True))
    both = jnp.maximum(touched[0] * touched[1], touched[2] * touched[3])
    zero = jnp.zeros((3, 128), f32)
    active = jnp.concatenate(found + [both, zero], axis=0)
    before = (down < along).astype(f32).astype(jnp.bfloat16)
    place_of = mul(active.astype(jnp.bfloat16), before)
    entries = lane + d_of * 128.0 + f_of * 4096.0 - float(dummy)
    entries = jnp.where(which < 4, entries, lane - float(blocks_f))
    spots = jnp.where(active > 0, place_of, -1.0)
    turned = jnp.transpose(jnp.concatenate([spots, entries] * 8, axis=0))
    rows = []
    for w in range(5):
        here = jnp.broadcast_to(turned[:, w : w + 1], square) == along
        given = jnp.broadcast_to(turned[:, 8 + w : 9 + w], square)
        rest = float(dummy if w < 4 else blocks_f)
        rows.append(jnp.sum(jnp.where(here, given, 0.0), axis=0, keepdims=True) + rest)
    lists[0:8, :] = jnp.concatenate(rows + [zero], axis=0).astype(jnp.int32)
    lists[8:16, :] = place_of.astype(jnp.int32)


def trips(lists):
    most = jnp.maximum(jnp.maximum(lists[8, 127], lists[9, 127]), jnp.maximum(lists[10, 127], lists[11, 127]))
    return (most + PER - 1) // PER


def act_trips(lists):
    return (lists[12, 127] + ACTS - 1) // ACTS


def prepare_weights(lists, raw, wide, w):
    count = raw.shape[2]

    def spread(t, carry):
        for which in range(4):
            copy, proj = divmod(which, 2)
            value = raw[copy, proj, :, pl.ds(pl.multiple_of(t * 128, 128), 128)].astype(jnp.float32)
            wide[which, pl.ds(2 * t, count, stride=PITCH), :] = value
            wide[which, pl.ds(2 * t + 1, count, stride=PITCH), :] = pltpu.roll(value, BLOCK, 1)
        return carry

    lax.fori_loop(0, BLOCK // 2, spread, 0, unroll=4)
    row = lax.broadcasted_iota(jnp.int32, (BLOCK, BLOCK), 0)
    col = lax.broadcasted_iota(jnp.int32, (BLOCK, BLOCK), 1)
    eye = (row == col).astype(jnp.float32).astype(jnp.bfloat16)

    def body(i):
        done = []
        for which in range(4):
            for u in range(PER):
                n = entry(lists, which, i + u)[0]
                block = wide[which, pl.ds(pl.multiple_of(n * PITCH, 8), BLOCK), :][:, :BLOCK].astype(jnp.bfloat16)
                done.append((which, n, block, mul_nt(eye, block)))
        for which, n, block, turned in done:
            w[0, which // 2, which % 2, n] = block
            w[1, which // 2, which % 2, n] = turned.astype(jnp.bfloat16)

    batched(trips(lists), PER, body)


def section_pass(lists, w, x, gy, pre, gh):
    def body(i):
        terms = []
        for copy in range(2):
            for u in range(PER):
                n, d, f = entry(lists, 2 * copy, i + u)
                terms.append((pre, f, mul(w[1, copy, 0, n], x[copy, d])))
                n, d, f = entry(lists, 2 * copy + 1, i + u)
                terms.append((gh, f, mul(w[0, copy, 1, n], gy[copy, d])))
        for ref, f, term in terms:
            ref[f] += term

    batched(trips(lists), PER, body)


def section_close(lists, w, hid, gp, out, first_fwd, first_bwd):
    lane = lax.broadcasted_iota(jnp.int32, (BLOCK, 128), 1) // 32
    fwd = [(lane == first_fwd + copy).astype(jnp.float32).astype(jnp.bfloat16) for copy in range(2)]
    bwd = [(lane == first_bwd + copy).astype(jnp.float32).astype(jnp.bfloat16) for copy in range(2)]

    def body(i):
        terms = []
        for copy in range(2):
            for u in range(PER):
                n, d, f = entry(lists, 2 * copy + 1, i + u)
                terms.append((d, mul(w[1, copy, 1, n], hid[f] * fwd[copy])))
                n, d, f = entry(lists, 2 * copy, i + u)
                terms.append((d, mul(w[0, copy, 0, n], gp[f] * bwd[copy])))
        for d, term in terms:
            out[d] += term

    batched(trips(lists), PER, body)


def clear(lists, refs):
    def body(i):
        for u in range(ACTS):
            f = lists[4, i + u]
            for ref in refs:
                ref[f] = jnp.zeros(ref.shape[1:], ref.dtype)

    batched(act_trips(lists), ACTS, body)


def first_kernel(
    pat, acts_in, cot_in, stash_in, raw, send_up, send_down, hid_out, gp_out, lists_out, w_out,
    acts, cot, stash, hid, gp, lists, wide, w, x, gy, pre, gh, out, sem,
):
    blocks_d, blocks_f = out.shape[0] - 1, pre.shape[0] - 1
    reads = [begin(acts_in, acts, sem.at[0]), begin(cot_in, cot, sem.at[1]), begin(stash_in, stash, sem.at[2])]
    build_lists(pat, lists_out, blocks_d, blocks_f)
    begin(lists_out, lists, sem.at[3]).wait()
    prepare_weights(lists, raw, wide, w)
    writes = [begin(w, w_out, sem.at[4])]
    clear(lists, (pre, gh))
    for read in reads:
        read.wait()
    masks = [copy_mask(copy, 128) for copy in range(2)]
    backward = lax.broadcasted_iota(jnp.int32, (128, 128), 1) >= 64

    def load(i, carry):
        cols = wide_columns(i)
        zero = jnp.zeros((64, 128), jnp.bfloat16)
        inputs = stack_tokens([acts[0, :, cols], acts[1, :, cols], stash[0, 0, :, cols], stash[1, 0, :, cols]])
        cots = stack_tokens([zero, cot[0, :, cols], cot[1, :, cols]])
        for copy in range(2):
            put(x, i, inputs * masks[copy], copy)
            put(gy, i, cots * masks[copy], copy)
        put(out, i, jnp.where(backward, cots.astype(jnp.float32), inputs.astype(jnp.float32)))
        return carry

    lax.fori_loop(0, blocks_d // 2, load, 0, unroll=2)
    section_pass(lists, w, x, gy, pre, gh)

    def act(i):
        for u in range(ACTS):
            f = lists[4, i + u]
            hidden, slope = gelu_parts(pre[f])
            hid[f] = hidden.astype(jnp.bfloat16)
            gp[f] = (slope * gh[f]).astype(jnp.bfloat16)

    batched(act_trips(lists), ACTS, act)
    writes += [begin(hid, hid_out, sem.at[5]), begin(gp, gp_out, sem.at[6])]
    section_close(lists, w, hid, gp, out, 0, 2)

    def store(i, carry):
        cols = wide_columns(i)
        value = jnp.concatenate([out[2 * i], out[2 * i + 1]], axis=0).astype(jnp.bfloat16).T
        send_up[0:32, cols] = value[0:32]
        send_up[32:64, cols] = value[96:128]
        send_down[:, cols] = value[32:96]
        return carry

    lax.fori_loop(0, blocks_d // 2, store, 0, unroll=4)
    for write in writes:
        write.wait()


def second_kernel(
    sections, lists, acts, cot, stash, entering, sent_up, sent_down, got_up, got_down, hid1_in, gp1_in, w_in,
    forward, backward, xs_out, gys_out, hid_out, gp_out,
    hid1, gp1, xs, gys, hid_both, gp_both, w, hid, x, gy, pre, gh, out, sem,
):
    fetch = begin(w_in, w, sem.at[0])
    early = [begin(hid1_in, hid1, sem.at[1]), begin(gp1_in, gp1, sem.at[2])]
    blocks_d, blocks_f = out.shape[0] - 1, pre.shape[0] - 1
    me = lax.axis_index("pipe")
    at_entry, at_exit = me == 0, me == sections - 1
    clear(lists, (pre, gh))

    def wipe(f, carry):
        hid_both[f] = jnp.zeros(hid_both.shape[1:], hid_both.dtype)
        gp_both[f] = jnp.zeros(gp_both.shape[1:], gp_both.dtype)
        return carry

    lax.fori_loop(0, blocks_f, wipe, 0, unroll=4)
    row = lax.broadcasted_iota(jnp.int32, (BLOCK, BLOCK), 0)
    col = lax.broadcasted_iota(jnp.int32, (BLOCK, BLOCK), 1)
    source = jnp.where(row < BLOCK // 2, 2 * row, 2 * row - BLOCK + 1)
    evens_first = (col == source).astype(jnp.float32).astype(jnp.bfloat16)
    masks = [copy_mask(copy, 128) for copy in range(2)]
    half_masks = [copy_mask(copy, BLOCK) for copy in range(2)]
    late = lax.broadcasted_iota(jnp.int32, (128, 128), 1) < 64
    late_half = lax.broadcasted_iota(jnp.int32, (BLOCK, 128), 1) < 64
    late_only = late.astype(jnp.float32).astype(jnp.bfloat16)

    def rearranged(value):
        return mul(evens_first, value).astype(jnp.bfloat16)

    def merged(first, second, mask):
        return jnp.where(mask, first.astype(jnp.float32), second.astype(jnp.float32))

    def load(i, carry):
        cols = wide_columns(i)
        x0 = jnp.where(at_entry, entering[0, :, cols], got_up[0:32, cols])
        x1 = jnp.where(at_exit, entering[1, :, cols], got_down[0:32, cols])
        g0 = jnp.where(at_exit, sent_up[0:32, cols], got_down[32:64, cols])
        g1 = jnp.where(at_entry, sent_down[0:32, cols], got_up[32:64, cols])
        s0 = jnp.where(at_exit, acts[0, :, cols], stash[0, 1, :, cols])
        s1 = jnp.where(at_entry, acts[1, :, cols], stash[1, 1, :, cols])
        inputs = stack_tokens([s0, s1, x0, x1])
        cots = stack_tokens([g0, g1, cot[0, :, cols], cot[1, :, cols]])
        saved = stack_tokens([s0, s1, stash[0, 0, :, cols], stash[1, 0, :, cols]])
        put(out, i, merged(cots, inputs, late))
        for copy in range(2):
            put(x, i, inputs * masks[copy], copy)
            put(gys, i, cots * masks[copy], copy)
            put(gy, i, cots * (masks[copy] * late_only), copy)
        for part in range(2):
            piece = rearranged(saved[part * BLOCK : (part + 1) * BLOCK])
            for copy in range(2):
                xs[copy, 2 * i + part] = piece * half_masks[copy]
        return carry

    lax.fori_loop(0, blocks_d // 2, load, 0, unroll=2)
    writes = [begin(xs, xs_out, sem.at[3]), begin(gys, gys_out, sem.at[4])]
    fetch.wait()
    section_pass(lists, w, x, gy, pre, gh)
    for read in early:
        read.wait()

    def act(i):
        for u in range(ACTS):
            f = lists[4, i + u]
            hidden, slope = gelu_parts(pre[f])
            hid[f] = hidden.astype(jnp.bfloat16)
            gp_both[f] = merged(slope * gh[f], gp1[f], late_half).astype(jnp.bfloat16)
            hid_both[f] = rearranged(merged(hidden, hid1[f], late_half).astype(jnp.bfloat16))

    batched(act_trips(lists), ACTS, act)
    writes += [begin(hid_both, hid_out, sem.at[5]), begin(gp_both, gp_out, sem.at[6])]
    section_close(lists, w, hid, gp_both, out, 2, 0)

    def store(i, carry):
        cols = wide_columns(i)
        value = jnp.concatenate([out[2 * i], out[2 * i + 1]], axis=0).astype(jnp.bfloat16).T
        for copy in range(2):
            backward[copy, :, cols] = value[32 * copy : 32 * copy + 32]
            forward[copy, :, cols] = value[64 + 32 * copy : 96 + 32 * copy]
        return carry

    lax.fori_loop(0, blocks_d // 2, store, 0, unroll=4)
    for write in writes:
        write.wait()


def two_wide(value):
    return jnp.concatenate([value[: BLOCK // 2], value[BLOCK // 2 :]], axis=1).astype(jnp.bfloat16)


def sum_kernel(
    sections, quarter, pat, xs, gys_in, hid_in, gp, total, gys, hid, local, grads, got_core, to_side, got_side, share, got_own, got_far, *sems
):
    core_sent, core_got, side_sent, side_got, own_sent, own_got, far_sent, far_got = sems
    blocks_d, blocks_f = xs.shape[1], gp.shape[0] - 1
    me, group = lax.axis_index("pipe"), lax.axis_index("dp")
    core, side = lax.rem(group, 2), group // 2
    near, over, far = group + 1 - 2 * core, group + 2 - 4 * side, sections - 1 - me
    reads = [begin(gys_in, gys, local.at[0]), begin(hid_in, hid, local.at[1])]
    barrier = pltpu.get_barrier_semaphore()
    for other in ((near, me), (over, me), (over, far)):
        pl.semaphore_signal(barrier, inc=1, device_id=other, device_id_type=pl.DeviceIdType.MESH)
    half = BLOCK // 2

    share_rows = quarter * half // PARTS

    def compute(j):
        copy, proj, part = j // (2 * PARTS), j // PARTS % 2, j % PARTS

        def step(q, carry):
            for u in range(quarter // PARTS):
                n = part * (quarter // PARTS) + u
                d, f = place(pat, copy, proj, q * quarter + n, blocks_d, blocks_f)
                if proj == 0:
                    value = mul_nt(xs[copy, d], gp[f])
                else:
                    value = mul_nt(hid[f], gys[copy, d])
                grads[j, q // 2, q % 2, u * half : (u + 1) * half] = two_wide(value)
            return carry

        lax.fori_loop(0, 4, step, 0)

    def copies(j):
        def remote(source, target, sent, got, to):
            return pltpu.make_async_remote_copy(
                src_ref=source, dst_ref=target, send_sem=sent.at[j], recv_sem=got.at[j],
                device_id=to, device_id_type=pl.DeviceIdType.MESH,
            )

        return (
            remote(grads.at[j, :, 1 - core], got_core.at[j], core_sent, core_got, (near, me)),
            remote(to_side.at[j], got_side.at[j], side_sent, side_got, (over, me)),
            remote(share.at[j], got_far.at[j], far_sent, far_got, (over, far)),
            remote(share.at[j], got_own.at[j], own_sent, own_got, (over, me)),
        )

    wires = [copies(j) for j in range(4 * PARTS)]

    def pieces(body):
        def step(i, carry):
            body(pl.ds(pl.multiple_of(i * 96, 96), 96))
            return carry

        lax.fori_loop(0, share_rows // 96, step, 0)

    def after_core(j):
        wires[j][0].wait_recv()

        def body(rows):
            value = grads[j, side, core, rows].astype(jnp.float32) + got_core[j, side, rows].astype(jnp.float32)
            to_side[j, rows] = value.astype(jnp.bfloat16)

        pieces(body)
        wires[j][1].start()

    def after_side(j):
        wires[j][1].wait_recv()

        def body(rows):
            value = grads[j, 1 - side, core, rows].astype(jnp.float32) + got_core[j, 1 - side, rows].astype(jnp.float32)
            share[j, rows] = (value + got_side[j, rows].astype(jnp.float32)).astype(jnp.bfloat16)

        pieces(body)
        wires[j][2].start()
        wires[j][3].start()

    def after_far(copy, proj, part):
        own, other = (copy * 2 + proj) * PARTS + part, ((1 - copy) * 2 + proj) * PARTS + part
        wires[own][3].wait_recv()
        wires[other][2].wait_recv()

        def body(i, carry):
            rows = pl.ds(pl.multiple_of(i * 96, 96), 96)
            value = got_own[own, rows].astype(jnp.float32) + got_far[other, rows].astype(jnp.float32)
            total[copy, pl.ds((part * share_rows + i * 96) * 2 + proj, 96, stride=2), :] = value
            return carry

        lax.fori_loop(0, share_rows // 96, body, 0)

    number = 4 * PARTS
    for step in range(number + 2):
        if step == PARTS:
            for read in reads:
                read.wait()
        if step < number:
            compute(step)
            if step == 0:
                pl.semaphore_wait(barrier, 3)
            wires[step][0].start()
        if 1 <= step < number + 1:
            after_core(step - 1)
        if 2 <= step:
            after_side(step - 2)
    for copy in (1, 0):
        for proj in range(2):
            for part in range(PARTS):
                after_far(copy, proj, part)
    for j in range(number):
        for wire in wires[j]:
            wire.wait_send()


def call(kernel, args, outs, scratch):
    space = {"s": pltpu.SMEM, "v": pltpu.VMEM, "a": pl.ANY}
    return pl.pallas_call(
        kernel,
        out_shape=[jax.ShapeDtypeStruct(*out[1:]) for out in outs],
        in_specs=[pl.BlockSpec(memory_space=space[kind]) for kind, _ in args],
        out_specs=[pl.BlockSpec(memory_space=space[out[0]]) for out in outs],
        scratch_shapes=[space[one[0]](*one[1:]) for one in scratch] + [pltpu.SemaphoreType.DMA((8,))],
        compiler_params=pltpu.CompilerParams(vmem_limit_bytes=VMEM_BYTES),
    )(*(value for _, value in args))


def dense(value):
    copies, projs, count, size = value.shape
    value = jnp.swapaxes(value, 1, 2).reshape(copies, count, projs, size // 128, 128)
    return jnp.swapaxes(value, 2, 3).reshape(copies, -1, 128)


def spread_out(value):
    value = value.reshape(2, -1, BLOCK // 2, 2, 128)
    count = value.shape[1]
    return jnp.swapaxes(jnp.swapaxes(value, 2, 3).reshape(2, count, 2, -1), 1, 2)


def shards(acts_in, cot_in, stash, entering, pattern, weights, momentum):
    bf16, f32 = jnp.bfloat16, jnp.float32
    me, sections = lax.axis_index("pipe"), lax.axis_size("pipe")
    group = lax.axis_index("dp")
    acts, cot, saved, fresh = (jnp.swapaxes(one, -1, -2) for one in (acts_in[0, 0], cot_in[0, 0], stash[0, 0], entering[0]))
    pat = jnp.concatenate(
        [
            lax.dynamic_index_in_dim(pattern, me, 0, keepdims=False),
            lax.dynamic_index_in_dim(pattern, sections - 1 - me, 0, keepdims=False),
        ]
    )
    pat = jnp.pad(pat, ((0, 4), (0, 128 - pat.shape[1])), constant_values=-1)
    tokens, width = acts.shape[1:]
    count = weights.shape[3]
    blocks_d, blocks_f = width // BLOCK, FF // BLOCK
    raw = weights[0]
    d_block, f_block = (blocks_d, BLOCK, 128), (blocks_f + 1, BLOCK, 128)
    x_block, out_block = (2, blocks_d + 1, BLOCK, 128), (blocks_d + 1, BLOCK, 128)
    w_shape = (2, 2, 2, count, BLOCK, BLOCK)
    send_up, send_down, hid, gp, lists, w = call(
        first_kernel,
        [("v", pat), ("a", acts), ("a", cot), ("a", saved), ("v", raw)],
        [
            ("v", (2 * tokens, width), bf16),
            ("v", (2 * tokens, width), bf16),
            ("a", f_block, bf16),
            ("a", f_block, bf16),
            ("v", (16, 128), jnp.int32),
            ("a", w_shape, bf16),
        ],
        [
            ("v", acts.shape, bf16),
            ("v", cot.shape, bf16),
            ("v", saved.shape, bf16),
            ("v", f_block, bf16),
            ("v", f_block, bf16),
            ("s", (16, 128), jnp.int32),
            ("v", (4, count * PITCH, 128), f32),
            ("v", w_shape, bf16),
            ("v", x_block, bf16),
            ("v", x_block, bf16),
            ("v", f_block, f32),
            ("v", f_block, f32),
            ("v", out_block, f32),
        ],
    )
    got_up = lax.ppermute(send_up, "pipe", [(i, i + 1) for i in range(sections - 1)])
    got_down = lax.ppermute(send_down, "pipe", [(i + 1, i) for i in range(sections - 1)])
    vectors = (acts, cot, saved, fresh, send_up, send_down, got_up, got_down)
    forward, backward, xs, gys, hid, gp = call(
        lambda *refs: second_kernel(sections, *refs),
        [("s", lists)] + [("v", one) for one in vectors] + [("a", hid), ("a", gp), ("a", w)],
        [("v", acts.shape, bf16)] * 2 + [("a", (2, *d_block), bf16)] * 2 + [("a", f_block, bf16)] * 2,
        [("v", f_block, bf16)] * 2
        + [("v", (2, *d_block), bf16)] * 2
        + [("v", f_block, bf16)] * 2
        + [
            ("v", w_shape, bf16),
            ("v", f_block, bf16),
            ("v", x_block, bf16),
            ("v", x_block, bf16),
            ("v", f_block, f32),
            ("v", f_block, f32),
            ("v", out_block, f32),
        ],
    )
    quarter = count // 4
    chunk = (4 * PARTS, quarter * BLOCK // 2 // PARTS, 128)
    smem, vmem = pl.BlockSpec(memory_space=pltpu.SMEM), pl.BlockSpec(memory_space=pltpu.VMEM)
    hbm = pl.BlockSpec(memory_space=pl.ANY)
    total = pl.pallas_call(
        lambda *refs: sum_kernel(sections, quarter, *refs),
        out_shape=jax.ShapeDtypeStruct((2, quarter * BLOCK, 128), f32),
        in_specs=[smem, vmem, hbm, hbm, vmem],
        out_specs=vmem,
        scratch_shapes=[
            pltpu.VMEM((2, *d_block), bf16),
            pltpu.VMEM(f_block, bf16),
            pltpu.SemaphoreType.DMA((2,)),
            pltpu.VMEM((4 * PARTS, 2, 2, *chunk[1:]), bf16),
            pltpu.VMEM((4 * PARTS, 2, *chunk[1:]), bf16),
            pltpu.VMEM(chunk, bf16),
            pltpu.VMEM(chunk, bf16),
            pltpu.VMEM(chunk, bf16),
            pltpu.VMEM(chunk, bf16),
            pltpu.VMEM(chunk, bf16),
        ]
        + [pltpu.SemaphoreType.DMA((4 * PARTS,))] * 8,
        compiler_params=pltpu.CompilerParams(collective_id=0, has_side_effects=True, vmem_limit_bytes=VMEM_BYTES),
    )(pat, xs, gys, hid, gp)
    own = lax.dynamic_slice_in_dim(weights[0], group * quarter, quarter, axis=2)
    momentum_next = BETA * dense(momentum[0]) + total / (2 * tokens)
    weights_next = spread_out((dense(own).astype(f32) - STEP * momentum_next).astype(bf16))
    momentum_next = spread_out(momentum_next)
    forward, backward = jnp.swapaxes(forward, 1, 2), jnp.swapaxes(backward, 1, 2)
    return forward[None, None], backward[None, None], weights_next[None], momentum_next[None]


def solution(mesh):
    placed = (
        P("dp", "pipe"),
        P("dp", "pipe"),
        P("dp", "pipe"),
        P("dp"),
        P(),
        P("pipe"),
        P("pipe", None, None, "dp"),
    )
    return jax.shard_map(
        shards,
        mesh=mesh,
        in_specs=placed,
        out_specs=(P("dp", "pipe"), P("dp", "pipe"), P("pipe", None, None, "dp"), P("pipe", None, None, "dp")),
        check_vma=False,
    )
```

```python
import jax
import jax.numpy as jnp
from jax import lax
from jax.experimental import pallas as pl
from jax.experimental.pallas import tpu as pltpu
from jax.sharding import PartitionSpec as P

FF = 6144
BLOCK = 64
BETA = 0.9
STEP = 0.2
PER = 12
ACTS = 8
PITCH = 72
PARTS = 2
VMEM_BYTES = 56 * 2**20


def dot(left, right, dims):
    return lax.dot_general(left, right, (dims, ((), ())), preferred_element_type=jnp.float32)


def mul(left, right):
    return dot(left, right, ((1,), (0,)))


def mul_nt(left, right):
    return dot(left, right, ((1,), (1,)))


def gelu_parts(values):
    cdf = 0.5 + 0.5 * lax.erf(values * 0.7071067811865476)
    slope = cdf + values * (0.3989422804014327 * jnp.exp(-0.5 * values * values))
    return values * cdf, slope


def stack_tokens(parts):
    return jnp.concatenate(parts, axis=0).T


def copy_mask(copy, rows):
    lane = lax.broadcasted_iota(jnp.int32, (rows, 128), 1) // 32
    return (lane % 2 == copy).astype(jnp.float32).astype(jnp.bfloat16)


def wide_columns(i):
    return pl.ds(pl.multiple_of(i * 128, 128), 128)


def put(ref, i, value, *lead):
    ref[(*lead, 2 * i)] = value[:BLOCK]
    ref[(*lead, 2 * i + 1)] = value[BLOCK:]


def place(pat, copy, proj, n, blocks_d, blocks_f):
    value = pat[16 + copy * 2 + proj, n]
    if proj == 0:
        r = value // blocks_f
        return r, value - r * blocks_f
    r = value // blocks_d
    return value - r * blocks_d, r


def entry(lists, which, i):
    value = lists[which, i]
    return value % 128, (value // 128) % 32, value // 4096


def batched(number, width, body):
    def step(i, carry):
        body(i * width)
        return carry

    lax.fori_loop(0, number, step, 0)


def begin(source, target, sem):
    copy = pltpu.make_async_copy(source, target, sem)
    copy.start()
    return copy


def build_lists(pat, lists, blocks_d, blocks_f):
    f32 = jnp.float32
    dummy = blocks_d * 128 + blocks_f * 4096
    value = pat.astype(f32)
    which = lax.broadcasted_iota(jnp.int32, (8, 128), 0)
    lane = lax.broadcasted_iota(jnp.int32, (8, 128), 1).astype(f32)
    width = jnp.where(which % 2 == 0, f32(blocks_f), f32(blocks_d))
    high = jnp.floor((value + 0.5) / width)
    low = value - high * width
    d_of, f_of = jnp.where(which % 2 == 0, high, low), jnp.where(which % 2 == 0, low, high)
    valid = value >= 0
    f_of = jnp.where(valid, f_of, -1.0 - which.astype(f32))
    f_down = jnp.transpose(jnp.concatenate([f_of] * 16, axis=0))
    square = (128, 128)
    along = lax.broadcasted_iota(jnp.int32, square, 1).astype(f32)
    down = lax.broadcasted_iota(jnp.int32, square, 0).astype(f32)
    found, touched = [], []
    for w in range(4):
        column = jnp.broadcast_to(f_down[:, (w ^ 1) : (w ^ 1) + 1], square)
        same = column == jnp.broadcast_to(f_of[w : w + 1], square)
        found.append(jnp.max(jnp.where(same, 1.0, 0.0), axis=0, keepdims=True))
        own = jnp.broadcast_to(f_down[:, w : w + 1], square) == along
        touched.append(jnp.max(jnp.where(own, 1.0, 0.0), axis=0, keepdims=True))
    both = jnp.maximum(touched[0] * touched[1], touched[2] * touched[3])
    zero = jnp.zeros((3, 128), f32)
    active = jnp.concatenate(found + [both, zero], axis=0)
    before = (down < along).astype(f32).astype(jnp.bfloat16)
    place_of = mul(active.astype(jnp.bfloat16), before)
    entries = lane + d_of * 128.0 + f_of * 4096.0 - float(dummy)
    entries = jnp.where(which < 4, entries, lane - float(blocks_f))
    spots = jnp.where(active > 0, place_of, -1.0)
    turned = jnp.transpose(jnp.concatenate([spots, entries] * 8, axis=0))
    rows = []
    for w in range(5):
        here = jnp.broadcast_to(turned[:, w : w + 1], square) == along
        given = jnp.broadcast_to(turned[:, 8 + w : 9 + w], square)
        rest = float(dummy if w < 4 else blocks_f)
        rows.append(jnp.sum(jnp.where(here, given, 0.0), axis=0, keepdims=True) + rest)
    lists[0:8, :] = jnp.concatenate(rows + [zero], axis=0).astype(jnp.int32)
    lists[8:16, :] = place_of.astype(jnp.int32)


def trips(lists):
    most = jnp.maximum(jnp.maximum(lists[8, 127], lists[9, 127]), jnp.maximum(lists[10, 127], lists[11, 127]))
    return (most + PER - 1) // PER


def act_trips(lists):
    return (lists[12, 127] + ACTS - 1) // ACTS


def prepare_weights(lists, raw, wide, w):
    count = raw.shape[2]

    def spread(t, carry):
        for which in range(4):
            copy, proj = divmod(which, 2)
            value = raw[copy, proj, :, pl.ds(pl.multiple_of(t * 128, 128), 128)].astype(jnp.float32)
            wide[which, pl.ds(2 * t, count, stride=PITCH), :] = value
            wide[which, pl.ds(2 * t + 1, count, stride=PITCH), :] = pltpu.roll(value, BLOCK, 1)
        return carry

    lax.fori_loop(0, BLOCK // 2, spread, 0, unroll=4)
    row = lax.broadcasted_iota(jnp.int32, (BLOCK, BLOCK), 0)
    col = lax.broadcasted_iota(jnp.int32, (BLOCK, BLOCK), 1)
    eye = (row == col).astype(jnp.float32).astype(jnp.bfloat16)

    def body(i):
        done = []
        for which in range(4):
            for u in range(PER):
                n = entry(lists, which, i + u)[0]
                block = wide[which, pl.ds(pl.multiple_of(n * PITCH, 8), BLOCK), :][:, :BLOCK].astype(jnp.bfloat16)
                done.append((which, n, block, mul_nt(eye, block)))
        for which, n, block, turned in done:
            w[0, which // 2, which % 2, n] = block
            w[1, which // 2, which % 2, n] = turned.astype(jnp.bfloat16)

    batched(trips(lists), PER, body)


def keep_own(wide, own, quarter):
    first, half = lax.axis_index("dp") * quarter, BLOCK // 2

    def step(n, carry):
        for which in range(4):
            copy, proj = divmod(which, 2)
            rows = wide[which, pl.ds(pl.multiple_of((first + n) * PITCH, 8), half, stride=2), :]
            own[copy, pl.ds(n * BLOCK + proj, half, stride=2), :] = rows
        return carry

    lax.fori_loop(0, quarter, step, 0, unroll=2)


def section_pass(lists, w, x, gy, pre, gh):
    def body(i):
        terms = []
        for copy in range(2):
            for u in range(PER):
                n, d, f = entry(lists, 2 * copy, i + u)
                terms.append((pre, f, mul(w[1, copy, 0, n], x[copy, d])))
                n, d, f = entry(lists, 2 * copy + 1, i + u)
                terms.append((gh, f, mul(w[0, copy, 1, n], gy[copy, d])))
        for ref, f, term in terms:
            ref[f] += term

    batched(trips(lists), PER, body)


def section_close(lists, w, hid, gp, out, first_fwd, first_bwd):
    lane = lax.broadcasted_iota(jnp.int32, (BLOCK, 128), 1) // 32
    fwd = [(lane == first_fwd + copy).astype(jnp.float32).astype(jnp.bfloat16) for copy in range(2)]
    bwd = [(lane == first_bwd + copy).astype(jnp.float32).astype(jnp.bfloat16) for copy in range(2)]

    def body(i):
        terms = []
        for copy in range(2):
            for u in range(PER):
                n, d, f = entry(lists, 2 * copy + 1, i + u)
                terms.append((d, mul(w[1, copy, 1, n], hid[f] * fwd[copy])))
                n, d, f = entry(lists, 2 * copy, i + u)
                terms.append((d, mul(w[0, copy, 0, n], gp[f] * bwd[copy])))
        for d, term in terms:
            out[d] += term

    batched(trips(lists), PER, body)


def clear(lists, refs):
    def body(i):
        for u in range(ACTS):
            f = lists[4, i + u]
            for ref in refs:
                ref[f] = jnp.zeros(ref.shape[1:], ref.dtype)

    batched(act_trips(lists), ACTS, body)


def first_kernel(
    sections, pattern, acts_in, cot_in, stash_in, raw_in, send_up, send_down, hid_out, gp_out, lists_out, w_out, own,
    acts, cot, stash, raw, hid, gp, lists, wide, w, x, gy, pre, gh, out, sem,
):
    blocks_d, blocks_f = out.shape[0] - 1, pre.shape[0] - 1
    reads = [begin(acts_in, acts, sem.at[0]), begin(cot_in, cot, sem.at[1]), begin(stash_in, stash, sem.at[2])]
    fetch = begin(raw_in, raw, sem.at[7])
    me, count = lax.axis_index("pipe"), raw.shape[2]
    lists_out[16:24, :] = jnp.full((8, 128), -1, jnp.int32)
    lists_out[16:18, 0:count] = pattern[me]
    lists_out[18:20, 0:count] = pattern[sections - 1 - me]
    build_lists(lists_out[16:24, :], lists_out, blocks_d, blocks_f)
    begin(lists_out, lists, sem.at[3]).wait()
    fetch.wait()
    prepare_weights(lists, raw, wide, w)
    writes = [begin(w, w_out, sem.at[4])]
    keep_own(wide, own, count // 4)
    clear(lists, (pre, gh))
    for read in reads:
        read.wait()
    masks = [copy_mask(copy, 128) for copy in range(2)]
    backward = lax.broadcasted_iota(jnp.int32, (128, 128), 1) >= 64

    def load(i, carry):
        cols = wide_columns(i)
        zero = jnp.zeros((64, 128), jnp.bfloat16)
        inputs = stack_tokens([acts[0, :, cols], acts[1, :, cols], stash[0, 0, :, cols], stash[1, 0, :, cols]])
        cots = stack_tokens([zero, cot[0, :, cols], cot[1, :, cols]])
        for copy in range(2):
            put(x, i, inputs * masks[copy], copy)
            put(gy, i, cots * masks[copy], copy)
        put(out, i, jnp.where(backward, cots.astype(jnp.float32), inputs.astype(jnp.float32)))
        return carry

    lax.fori_loop(0, blocks_d // 2, load, 0, unroll=2)
    section_pass(lists, w, x, gy, pre, gh)

    def act(i):
        for u in range(ACTS):
            f = lists[4, i + u]
            hidden, slope = gelu_parts(pre[f])
            hid[f] = hidden.astype(jnp.bfloat16)
            gp[f] = (slope * gh[f]).astype(jnp.bfloat16)

    batched(act_trips(lists), ACTS, act)
    writes += [begin(hid, hid_out, sem.at[5]), begin(gp, gp_out, sem.at[6])]
    section_close(lists, w, hid, gp, out, 0, 2)

    def store(i, carry):
        cols = wide_columns(i)
        value = jnp.concatenate([out[2 * i], out[2 * i + 1]], axis=0).astype(jnp.bfloat16).T
        send_up[0:32, cols] = value[0:32]
        send_up[32:64, cols] = value[96:128]
        send_down[:, cols] = value[32:96]
        return carry

    lax.fori_loop(0, blocks_d // 2, store, 0, unroll=4)
    for write in writes:
        write.wait()


def second_kernel(
    sections, lists, acts, cot, stash, entering, sent_up, sent_down, got_up, got_down, hid1_in, gp1_in, w_in,
    forward, backward, xs_out, gys_out, hid_out, gp_out,
    hid1, gp1, xs, gys, hid_both, gp_both, w, hid, x, gy, pre, gh, out, sem,
):
    fetch = begin(w_in, w, sem.at[0])
    early = [begin(hid1_in, hid1, sem.at[1]), begin(gp1_in, gp1, sem.at[2])]
    blocks_d, blocks_f = out.shape[0] - 1, pre.shape[0] - 1
    me = lax.axis_index("pipe")
    at_entry, at_exit = me == 0, me == sections - 1
    clear(lists, (pre, gh))

    def wipe(f, carry):
        hid_both[f] = jnp.zeros(hid_both.shape[1:], hid_both.dtype)
        gp_both[f] = jnp.zeros(gp_both.shape[1:], gp_both.dtype)
        return carry

    lax.fori_loop(0, blocks_f, wipe, 0, unroll=4)
    row = lax.broadcasted_iota(jnp.int32, (BLOCK, BLOCK), 0)
    col = lax.broadcasted_iota(jnp.int32, (BLOCK, BLOCK), 1)
    source = jnp.where(row < BLOCK // 2, 2 * row, 2 * row - BLOCK + 1)
    evens_first = (col == source).astype(jnp.float32).astype(jnp.bfloat16)
    masks = [copy_mask(copy, 128) for copy in range(2)]
    half_masks = [copy_mask(copy, BLOCK) for copy in range(2)]
    late = lax.broadcasted_iota(jnp.int32, (128, 128), 1) < 64
    late_half = lax.broadcasted_iota(jnp.int32, (BLOCK, 128), 1) < 64
    late_only = late.astype(jnp.float32).astype(jnp.bfloat16)

    def rearranged(value):
        return mul(evens_first, value).astype(jnp.bfloat16)

    def merged(first, second, mask):
        return jnp.where(mask, first.astype(jnp.float32), second.astype(jnp.float32))

    def load(i, carry):
        cols = wide_columns(i)
        x0 = jnp.where(at_entry, entering[0, :, cols], got_up[0:32, cols])
        x1 = jnp.where(at_exit, entering[1, :, cols], got_down[0:32, cols])
        g0 = jnp.where(at_exit, sent_up[0:32, cols], got_down[32:64, cols])
        g1 = jnp.where(at_entry, sent_down[0:32, cols], got_up[32:64, cols])
        s0 = jnp.where(at_exit, acts[0, :, cols], stash[0, 1, :, cols])
        s1 = jnp.where(at_entry, acts[1, :, cols], stash[1, 1, :, cols])
        inputs = stack_tokens([s0, s1, x0, x1])
        cots = stack_tokens([g0, g1, cot[0, :, cols], cot[1, :, cols]])
        saved = stack_tokens([s0, s1, stash[0, 0, :, cols], stash[1, 0, :, cols]])
        put(out, i, merged(cots, inputs, late))
        for copy in range(2):
            put(x, i, inputs * masks[copy], copy)
            put(gys, i, cots * masks[copy], copy)
            put(gy, i, cots * (masks[copy] * late_only), copy)
        for part in range(2):
            piece = rearranged(saved[part * BLOCK : (part + 1) * BLOCK])
            for copy in range(2):
                xs[copy, 2 * i + part] = piece * half_masks[copy]
        return carry

    lax.fori_loop(0, blocks_d // 2, load, 0, unroll=2)
    writes = [begin(xs, xs_out, sem.at[3]), begin(gys, gys_out, sem.at[4])]
    fetch.wait()
    section_pass(lists, w, x, gy, pre, gh)
    for read in early:
        read.wait()

    def act(i):
        for u in range(ACTS):
            f = lists[4, i + u]
            hidden, slope = gelu_parts(pre[f])
            hid[f] = hidden.astype(jnp.bfloat16)
            gp_both[f] = merged(slope * gh[f], gp1[f], late_half).astype(jnp.bfloat16)
            hid_both[f] = rearranged(merged(hidden, hid1[f], late_half).astype(jnp.bfloat16))

    batched(act_trips(lists), ACTS, act)
    writes += [begin(hid_both, hid_out, sem.at[5]), begin(gp_both, gp_out, sem.at[6])]
    section_close(lists, w, hid, gp_both, out, 2, 0)

    def store(i, carry):
        cols = wide_columns(i)
        value = jnp.concatenate([out[2 * i], out[2 * i + 1]], axis=0).astype(jnp.bfloat16).T
        for copy in range(2):
            backward[copy, :, cols] = value[32 * copy : 32 * copy + 32]
            forward[copy, :, cols] = value[64 + 32 * copy : 96 + 32 * copy]
        return carry

    lax.fori_loop(0, blocks_d // 2, store, 0, unroll=4)
    for write in writes:
        write.wait()


def swap_kernel(sections, up, down, got_up, got_down, sent, got):
    me, group = lax.axis_index("pipe"), lax.axis_index("dp")
    after, before = lax.rem(me + 1, sections), lax.rem(me + sections - 1, sections)
    barrier = pltpu.get_barrier_semaphore()
    for other in (after, before):
        pl.semaphore_signal(barrier, inc=1, device_id=(group, other), device_id_type=pl.DeviceIdType.MESH)
    pl.semaphore_wait(barrier, 2)
    wires = [
        pltpu.make_async_remote_copy(
            src_ref=source, dst_ref=target, send_sem=sent.at[i], recv_sem=got.at[i],
            device_id=(group, to), device_id_type=pl.DeviceIdType.MESH,
        )
        for i, (source, target, to) in enumerate(((up, got_up, after), (down, got_down, before)))
    ]
    for wire in wires:
        wire.start()
    for wire in wires:
        wire.wait()


def two_wide(value):
    return jnp.concatenate([value[: BLOCK // 2], value[BLOCK // 2 :]], axis=1).astype(jnp.bfloat16)


def sum_kernel(
    sections, quarter, pat, xs, gys_in, hid_in, gp, total, gys, hid, local, grads, got_core, to_side, got_side, share, got_own, got_far, *sems
):
    core_sent, core_got, side_sent, side_got, own_sent, own_got, far_sent, far_got = sems
    blocks_d, blocks_f = xs.shape[1], gp.shape[0] - 1
    me, group = lax.axis_index("pipe"), lax.axis_index("dp")
    core, side = lax.rem(group, 2), group // 2
    near, over, far = group + 1 - 2 * core, group + 2 - 4 * side, sections - 1 - me
    reads = [begin(gys_in, gys, local.at[0]), begin(hid_in, hid, local.at[1])]
    barrier = pltpu.get_barrier_semaphore()
    for other in ((near, me), (over, me), (over, far)):
        pl.semaphore_signal(barrier, inc=1, device_id=other, device_id_type=pl.DeviceIdType.MESH)
    half = BLOCK // 2

    share_rows = quarter * half // PARTS

    def compute(j):
        copy, proj, part = j // (2 * PARTS), j // PARTS % 2, j % PARTS

        def step(q, carry):
            for u in range(quarter // PARTS):
                n = part * (quarter // PARTS) + u
                d, f = place(pat, copy, proj, q * quarter + n, blocks_d, blocks_f)
                if proj == 0:
                    value = mul_nt(xs[copy, d], gp[f])
                else:
                    value = mul_nt(hid[f], gys[copy, d])
                grads[j, q // 2, q % 2, u * half : (u + 1) * half] = two_wide(value)
            return carry

        lax.fori_loop(0, 4, step, 0)

    def copies(j):
        def remote(source, target, sent, got, to):
            return pltpu.make_async_remote_copy(
                src_ref=source, dst_ref=target, send_sem=sent.at[j], recv_sem=got.at[j],
                device_id=to, device_id_type=pl.DeviceIdType.MESH,
            )

        return (
            remote(grads.at[j, :, 1 - core], got_core.at[j], core_sent, core_got, (near, me)),
            remote(to_side.at[j], got_side.at[j], side_sent, side_got, (over, me)),
            remote(share.at[j], got_far.at[j], far_sent, far_got, (over, far)),
            remote(share.at[j], got_own.at[j], own_sent, own_got, (over, me)),
        )

    wires = [copies(j) for j in range(4 * PARTS)]

    def pieces(body):
        def step(i, carry):
            body(pl.ds(pl.multiple_of(i * 96, 96), 96))
            return carry

        lax.fori_loop(0, share_rows // 96, step, 0)

    def after_core(j):
        wires[j][0].wait_recv()

        def body(rows):
            value = grads[j, side, core, rows].astype(jnp.float32) + got_core[j, side, rows].astype(jnp.float32)
            to_side[j, rows] = value.astype(jnp.bfloat16)

        pieces(body)
        wires[j][1].start()

    def after_side(j):
        wires[j][1].wait_recv()

        def body(rows):
            value = grads[j, 1 - side, core, rows].astype(jnp.float32) + got_core[j, 1 - side, rows].astype(jnp.float32)
            share[j, rows] = (value + got_side[j, rows].astype(jnp.float32)).astype(jnp.bfloat16)

        pieces(body)
        wires[j][2].start()
        wires[j][3].start()

    def after_far(copy, proj, part):
        own, other = (copy * 2 + proj) * PARTS + part, ((1 - copy) * 2 + proj) * PARTS + part
        wires[own][3].wait_recv()
        wires[other][2].wait_recv()

        def body(i, carry):
            rows = pl.ds(pl.multiple_of(i * 96, 96), 96)
            value = got_own[own, rows].astype(jnp.float32) + got_far[other, rows].astype(jnp.float32)
            total[copy, pl.ds((part * share_rows + i * 96) * 2 + proj, 96, stride=2), :] = value
            return carry

        lax.fori_loop(0, share_rows // 96, body, 0)

    number = 4 * PARTS
    for step in range(number + 2):
        if step == PARTS:
            for read in reads:
                read.wait()
        if step < number:
            compute(step)
            if step == 0:
                pl.semaphore_wait(barrier, 3)
            wires[step][0].start()
        if 1 <= step < number + 1:
            after_core(step - 1)
        if 2 <= step:
            after_side(step - 2)
    for copy in (1, 0):
        for proj in range(2):
            for part in range(PARTS):
                after_far(copy, proj, part)
    for j in range(number):
        for wire in wires[j]:
            wire.wait_send()


def call(kernel, args, outs, scratch):
    space = {"s": pltpu.SMEM, "v": pltpu.VMEM, "a": pl.ANY}
    return pl.pallas_call(
        kernel,
        out_shape=[jax.ShapeDtypeStruct(*out[1:]) for out in outs],
        in_specs=[pl.BlockSpec(memory_space=space[kind]) for kind, _ in args],
        out_specs=[pl.BlockSpec(memory_space=space[out[0]]) for out in outs],
        scratch_shapes=[space[one[0]](*one[1:]) for one in scratch] + [pltpu.SemaphoreType.DMA((8,))],
        compiler_params=pltpu.CompilerParams(vmem_limit_bytes=VMEM_BYTES),
    )(*(value for _, value in args))


def dense(value):
    copies, projs, count, size = value.shape
    value = jnp.swapaxes(value, 1, 2).reshape(copies, count, projs, size // 128, 128)
    return jnp.swapaxes(value, 2, 3).reshape(copies, -1, 128)


def spread_out(value):
    value = value.reshape(2, -1, BLOCK // 2, 2, 128)
    count = value.shape[1]
    return jnp.swapaxes(jnp.swapaxes(value, 2, 3).reshape(2, count, 2, -1), 1, 2)


def shards(acts_in, cot_in, stash, entering, pattern, weights, momentum):
    bf16, f32 = jnp.bfloat16, jnp.float32
    sections = lax.axis_size("pipe")
    acts, cot, saved, fresh = (jnp.swapaxes(one, -1, -2) for one in (acts_in[0, 0], cot_in[0, 0], stash[0, 0], entering[0]))
    tokens, width = acts.shape[1:]
    count = weights.shape[3]
    blocks_d, blocks_f = width // BLOCK, FF // BLOCK
    raw = weights[0]
    d_block, f_block = (blocks_d, BLOCK, 128), (blocks_f + 1, BLOCK, 128)
    x_block, out_block = (2, blocks_d + 1, BLOCK, 128), (blocks_d + 1, BLOCK, 128)
    w_shape = (2, 2, 2, count, BLOCK, BLOCK)
    send_up, send_down, hid, gp, lists, w, own = call(
        lambda *refs: first_kernel(sections, *refs),
        [("v", pattern), ("a", acts), ("a", cot), ("a", saved), ("a", raw)],
        [
            ("v", (2 * tokens, width), bf16),
            ("v", (2 * tokens, width), bf16),
            ("a", f_block, bf16),
            ("a", f_block, bf16),
            ("v", (24, 128), jnp.int32),
            ("a", w_shape, bf16),
            ("v", (2, count // 4 * BLOCK, 128), f32),
        ],
        [
            ("v", acts.shape, bf16),
            ("v", cot.shape, bf16),
            ("v", saved.shape, bf16),
            ("v", raw.shape, bf16),
            ("v", f_block, bf16),
            ("v", f_block, bf16),
            ("s", (24, 128), jnp.int32),
            ("v", (4, count * PITCH, 128), f32),
            ("v", w_shape, bf16),
            ("v", x_block, bf16),
            ("v", x_block, bf16),
            ("v", f_block, f32),
            ("v", f_block, f32),
            ("v", out_block, f32),
        ],
    )
    got_up, got_down = pl.pallas_call(
        lambda *refs: swap_kernel(sections, *refs),
        out_shape=[jax.ShapeDtypeStruct(send_up.shape, bf16)] * 2,
        in_specs=[pl.BlockSpec(memory_space=pltpu.VMEM)] * 2,
        out_specs=[pl.BlockSpec(memory_space=pltpu.VMEM)] * 2,
        scratch_shapes=[pltpu.SemaphoreType.DMA((2,))] * 2,
        compiler_params=pltpu.CompilerParams(collective_id=1, has_side_effects=True),
    )(send_up, send_down)
    vectors = (acts, cot, saved, fresh, send_up, send_down, got_up, got_down)
    forward, backward, xs, gys, hid, gp = call(
        lambda *refs: second_kernel(sections, *refs),
        [("s", lists)] + [("v", one) for one in vectors] + [("a", hid), ("a", gp), ("a", w)],
        [("v", acts.shape, bf16)] * 2 + [("a", (2, *d_block), bf16)] * 2 + [("a", f_block, bf16)] * 2,
        [("v", f_block, bf16)] * 2
        + [("v", (2, *d_block), bf16)] * 2
        + [("v", f_block, bf16)] * 2
        + [
            ("v", w_shape, bf16),
            ("v", f_block, bf16),
            ("v", x_block, bf16),
            ("v", x_block, bf16),
            ("v", f_block, f32),
            ("v", f_block, f32),
            ("v", out_block, f32),
        ],
    )
    quarter = count // 4
    chunk = (4 * PARTS, quarter * BLOCK // 2 // PARTS, 128)
    smem, vmem = pl.BlockSpec(memory_space=pltpu.SMEM), pl.BlockSpec(memory_space=pltpu.VMEM)
    hbm = pl.BlockSpec(memory_space=pl.ANY)
    total = pl.pallas_call(
        lambda *refs: sum_kernel(sections, quarter, *refs),
        out_shape=jax.ShapeDtypeStruct((2, quarter * BLOCK, 128), f32),
        in_specs=[smem, vmem, hbm, hbm, vmem],
        out_specs=vmem,
        scratch_shapes=[
            pltpu.VMEM((2, *d_block), bf16),
            pltpu.VMEM(f_block, bf16),
            pltpu.SemaphoreType.DMA((2,)),
            pltpu.VMEM((4 * PARTS, 2, 2, *chunk[1:]), bf16),
            pltpu.VMEM((4 * PARTS, 2, *chunk[1:]), bf16),
            pltpu.VMEM(chunk, bf16),
            pltpu.VMEM(chunk, bf16),
            pltpu.VMEM(chunk, bf16),
            pltpu.VMEM(chunk, bf16),
            pltpu.VMEM(chunk, bf16),
        ]
        + [pltpu.SemaphoreType.DMA((4 * PARTS,))] * 8,
        compiler_params=pltpu.CompilerParams(collective_id=0, has_side_effects=True, vmem_limit_bytes=VMEM_BYTES),
    )(lists, xs, gys, hid, gp)
    momentum_next = BETA * dense(momentum[0]) + total / (2 * tokens)
    weights_next = spread_out((own - STEP * momentum_next).astype(bf16))
    momentum_next = spread_out(momentum_next)
    forward, backward = jnp.swapaxes(forward, 1, 2), jnp.swapaxes(backward, 1, 2)
    return forward[None, None], backward[None, None], weights_next[None], momentum_next[None]


def solution(mesh):
    placed = (
        P("dp", "pipe"),
        P("dp", "pipe"),
        P("dp", "pipe"),
        P("dp"),
        P(),
        P("pipe"),
        P("pipe", None, None, "dp"),
    )
    return jax.shard_map(
        shards,
        mesh=mesh,
        in_specs=placed,
        out_specs=(P("dp", "pipe"), P("dp", "pipe"), P("pipe", None, None, "dp"), P("pipe", None, None, "dp")),
        check_vma=False,
    )
```
